256 devices in a mesh: row: 16 (over z, y_lo), col: 16 (over y_hi, x, core).
Axes of the slice: x: 4, y: 4 (y_hi: 2, y_lo: 2; y = y_hi * 2 + y_lo), z: 8, core: 2. Of those that a mesh axis runs over, the one named last changes fastest.
Arguments:
- pair: bfloat16 [1536, 1536, 128], P('row', 'col'), may hold values from -6 to 6
- residue_mask: int32 [1536], replicated, may hold values 0 or 1
- norm_gain: float32 [128], replicated, may hold values from 0.1 to 1.9
- w_in: bfloat16 [128, 512], replicated, may hold values from -0.5 to 0.5
- b_in: float32 [512], replicated, may hold values from -3 to 3
- w_gate: bfloat16 [128, 128], replicated, may hold values from -0.5 to 0.5
- b_gate: float32 [128], replicated, may hold values from -3 to 3
- out_gain: float32 [128], replicated, may hold values from 0.1 to 1.9
- w_out: bfloat16 [128, 128], replicated, may hold values from -0.5 to 0.5
- b_out: float32 [128], replicated, may hold values from -3 to 3
Outputs:
- update: bfloat16 [1536, 1536, 128], P('row', 'col')
The draws below stay inside these ranges and needn't reach their ends.
All inputs are finite; a program needn't handle non-finite values.
Results may differ from the reference program's by a relative error of at most 0.015.
Values may be sent and summed in bfloat16 or wider, within the bound.
A program may use at most 64 MiB of HBM per device.

```python
import jax
import jax.numpy as jnp
from jax import lax

CZ = 128
C = 128
N = 1536


def with_ends(values, stream_key, smallest, high):
    longest = values.shape.index(max(values.shape))
    spots = []
    for shift in (0, 1):
        where = [jax.random.randint(jax.random.fold_in(stream_key, axis), (), 0, length) for axis, length in enumerate(values.shape)]
        where[longest] = (where[longest] + shift) % values.shape[longest]
        spots.append(tuple(where))
    return values.at[spots[0]].set(smallest).at[spots[1]].set(high)


def block_levels(rng, extent, pieces, least, largest):
    factor_of, own = 1.0, jax.random.fold_in(rng, 6)
    for dim, blocks in pieces:
        draws = jnp.exp(jax.random.uniform(jax.random.fold_in(own, dim), (blocks,), jnp.float32, least / len(pieces), largest / len(pieces)))
        factor_of = factor_of * jnp.repeat(draws, extent[dim] // blocks).reshape([-1 if axis == dim else 1 for axis in range(len(extent))])
    return factor_of


def normal_values(key, dims, spread, limit, cuts=(), kind=jnp.bfloat16):
    level = block_levels(key, dims, cuts, -0.22, 0.18) if cuts else 1.0
    entries = jax.random.normal(key, dims, jnp.float32) * spread * level
    return jnp.minimum(jnp.maximum(entries, -limit), limit).astype(kind)


def setup_inputs(seed: int = 0) -> dict:
    splits = jax.random.split(jax.random.key(seed), 11)
    return {
        "pair": normal_values(splits[0], (N, N, CZ), 1.0, 6.0, ((0, 16), (1, 16))),
        "residue_mask": with_ends((jax.random.randint(splits[1], (N,), 0, 8) < 7).astype(jnp.int32), jax.random.fold_in(splits[1], 1), 0, 1),
        "norm_gain": jnp.clip(1.0 + 0.18 * jax.random.normal(splits[2], (CZ,), jnp.float32), 0.1, 1.9),
        "w_in": normal_values(splits[3], (CZ, 4 * C), CZ ** -0.5, 0.5),
        "b_in": normal_values(splits[4], (4 * C,), 0.5, 3.0, (), jnp.float32),
        "w_gate": normal_values(splits[5], (CZ, CZ), CZ ** -0.5, 0.5),
        "b_gate": normal_values(splits[6], (CZ,), 0.5, 3.0, (), jnp.float32),
        "out_gain": jnp.clip(1.0 + 0.18 * jax.random.normal(splits[7], (C,), jnp.float32), 0.1, 1.9),
        "w_out": normal_values(splits[8], (C, CZ), C ** -0.5, 0.5),
        "b_out": normal_values(splits[9], (CZ,), 0.5, 3.0, (), jnp.float32),
    }


def layer_norm(values, gain):
    mean = lax.optimization_barrier(jnp.mean(values, axis=-1, keepdims=True))
    centred = values - mean
    var = lax.optimization_barrier(jnp.mean(centred * centred, axis=-1, keepdims=True))
    return centred * lax.rsqrt(var + 1e-05) * gain

def reference(pair, residue_mask, norm_gain, w_in, b_in, w_gate, b_gate, out_gain, w_out, b_out):
    blocks = 16
    height = N // blocks
    valid = residue_mask.astype(jnp.float32)
    starts = jnp.arange(blocks, dtype=jnp.int32)

    def normed_rows(index):
        rows = lax.dynamic_slice_in_dim(pair, index * height, height, 0)
        return layer_norm(rows.astype(jnp.float32), norm_gain).astype(jnp.bfloat16)

    def front(index):
        normed = normed_rows(index)
        proj = jnp.dot(normed.reshape(height * N, CZ), w_in, preferred_element_type=jnp.float32) + b_in
        proj = proj.reshape(height, N, 4 * C)
        row_valid = lax.dynamic_slice_in_dim(valid, index * height, height, 0)
        pair_mask = (row_valid[:, None] * valid[None, :])[:, :, None]
        a_proj = (pair_mask * jax.nn.sigmoid(proj[:, :, C:2 * C]) * proj[:, :, :C]).astype(jnp.bfloat16)
        b_proj = (pair_mask * jax.nn.sigmoid(proj[:, :, 3 * C:]) * proj[:, :, 2 * C:3 * C]).astype(jnp.bfloat16)
        return (a_proj.transpose(2, 0, 1), b_proj.transpose(2, 0, 1))
    a_blocks, b_blocks = lax.map(front, starts)
    a_chan = a_blocks.transpose(1, 0, 2, 3).reshape(C, N, N)
    b_chan = b_blocks.transpose(1, 0, 2, 3).reshape(C, N, N)

    def channel_product(operands):
        return jnp.dot(operands[0], operands[1].T, preferred_element_type=jnp.float32)
    prod = lax.map(channel_product, (a_chan, b_chan))

    def back(index):
        normed = normed_rows(index)
        block = lax.dynamic_slice_in_dim(prod, index * height, height, 1).transpose(1, 2, 0)
        prod_norm = layer_norm(block, out_gain).astype(jnp.bfloat16)
        linear = jnp.dot(prod_norm.reshape(height * N, C), w_out, preferred_element_type=jnp.float32) + b_out
        gating = jax.nn.sigmoid(jnp.dot(normed.reshape(height * N, CZ), w_gate, preferred_element_type=jnp.float32) + b_gate)
        return (gating * linear).reshape(height, N, CZ).astype(jnp.bfloat16)
    return lax.map(back, starts).reshape(N, N, CZ)
```

```python
import functools

import jax
import jax.numpy as jnp
from jax import lax
from jax.experimental import pallas as pl
from jax.experimental.pallas import tpu as pltpu
from jax.sharding import PartitionSpec as P

MESH = pl.DeviceIdType.MESH
BF16 = jnp.bfloat16
F32 = jnp.float32
LANES = 128


def join4(parts):
    lane = lax.broadcasted_iota(jnp.int32, parts[0].shape, 1)
    one, two, three = (pltpu.roll(parts[n], 128 - 32 * n, 1) for n in (1, 2, 3))
    return (
        jnp.where(lane < 96, parts[0], one),
        jnp.where(lane < 64, one, two),
        jnp.where(lane < 32, two, three),
    )


def split4(parts):
    lane = lax.broadcasted_iota(jnp.int32, parts[0].shape, 1)
    first, second, third = parts
    return (
        first,
        jnp.where(lane < 32, pltpu.roll(first, 32, 1), pltpu.roll(second, 32, 1)),
        jnp.where(lane < 64, pltpu.roll(second, 64, 1), pltpu.roll(third, 64, 1)),
        pltpu.roll(third, 96, 1),
    )


def triangle_kernel(
    nz, nch, ci, ab, out, recv1, zs, za, zb, other, prods, back, un, s1, r1, s2, r2a, r2b, so, ro, s3, r3, s4, r4
):
    nq = 2 * nz
    row, col = lax.axis_index("row"), lax.axis_index("col")
    z, yl = row // 2, row % 2
    w, core = col // 2, col % 2
    mine = yl * nz + w

    barrier = pltpu.get_barrier_semaphore()

    def greet_plane(t, _):
        dev = lax.rem(yl * nq + col + t, 2 * nq)
        pl.semaphore_signal(
            barrier, inc=1, device_id=(2 * z + dev // nq, dev % nq), device_id_type=MESH
        )
        return 0

    lax.fori_loop(1, 2 * nq, greet_plane, 0)

    def greet_line(t, _):
        pl.semaphore_signal(
            barrier, inc=1, device_id=(2 * lax.rem(z + t, nz) + yl, col), device_id_type=MESH
        )
        return 0

    lax.fori_loop(1, nz, greet_line, 0)
    pl.semaphore_wait(barrier, 2 * nq - 1 + nz - 1)

    def send1(arr, m):
        def step(t, _):
            p = lax.rem(mine + t, nq)
            here = jnp.logical_and(p == mine, core == yl)

            @pl.when(here)
            def _():
                pltpu.make_async_copy(ab.at[arr, m, p], recv1.at[arr, m, col], r1.at[arr, m]).start()

            @pl.when(jnp.logical_not(here))
            def _():
                pltpu.make_async_remote_copy(
                    src_ref=ab.at[arr, m, p],
                    dst_ref=recv1.at[arr, m, col],
                    send_sem=s1,
                    recv_sem=r1.at[arr, m],
                    device_id=(2 * z + p // nz, 2 * (p % nz) + yl),
                    device_id_type=MESH,
                ).start()

            return 0

        lax.fori_loop(0, nq, step, 0)

    def wait_all(ref, sem):
        pltpu.make_async_copy(ref, ref, sem).wait()

    def send_line(src, dst, target, send_sem, recv_sem):
        @pl.when(target == z)
        def _():
            pltpu.make_async_copy(src, dst, recv_sem).start()

        @pl.when(target != z)
        def _():
            pltpu.make_async_remote_copy(
                src_ref=src,
                dst_ref=dst,
                send_sem=send_sem,
                recv_sem=recv_sem,
                device_id=(2 * target + yl, col),
                device_id_type=MESH,
            ).start()

    def join_and_send(arr, m):
        def step(t, _):
            ch = lax.rem(z + 1 + t, nz)
            for g in range(nq // 4):
                blocks = join4([recv1[arr, m, 4 * g + n, ch].astype(F32) for n in range(4)])
                for n in range(3):
                    zs[arr, m, ch, :, (3 * g + n) * LANES : (3 * g + n + 1) * LANES] = blocks[
                        n
                    ].astype(BF16)
            if arr == 0:
                send_line(zs.at[0, m, ch], za.at[m, z], ch, s2, r2a.at[m])
            else:
                send_line(zs.at[1, m, ch], zb.at[z, m * ci : (m + 1) * ci], ch, s2, r2b)
            return 0

        lax.fori_loop(0, nz, step, 0)

    order = [(1, m) for m in range(nch)] + [(0, m) for m in range(nch)]
    send1(*order[0])
    send1(*order[1])
    for n, (arr, m) in enumerate(order):
        wait_all(recv1.at[arr, m], r1.at[arr, m])
        if n + 2 < len(order):
            send1(*order[n + 2])
        join_and_send(arr, m)

    ti = nch * ci
    wait_all(zb, r2b)

    def multiply(lhs_ref, m, h):
        lhs = lhs_ref[...].reshape(nz * ci, lhs_ref.shape[-1])

        def step(g, _):
            rhs = zb[pl.ds(4 * g, 4)].reshape(4 * ti, zb.shape[-1])
            res = lax.dot_general(lhs, rhs, (((1,), (1,)), ((), ())), preferred_element_type=F32)
            prods[m, :, h, g] = res.reshape(nz, ci, 4 * ti).astype(BF16)
            return 0

        lax.fori_loop(0, nz // 4, step, 0)

    def swap(m):
        return pltpu.make_async_remote_copy(
            src_ref=za.at[m],
            dst_ref=other.at[m],
            send_sem=so.at[m],
            recv_sem=ro.at[m],
            device_id=(row, 2 * w + 1 - core),
            device_id_type=MESH,
        )

    def send_products(m):
        def step(t, _):
            target = lax.rem(z + 1 + t, nz)
            send_line(prods.at[m, target], back.at[m, z], target, s3, r3.at[m])
            return 0

        lax.fori_loop(0, nz, step, 0)

    def split_and_send(m):
        wait_all(back.at[m], r3.at[m])

        def step(ch, _):
            for h in range(2):
                for g in range(nz // 4):
                    blocks = split4(
                        [
                            back[m, ch, h, g, :, n * LANES : (n + 1) * LANES].astype(F32)
                            for n in range(3)
                        ]
                    )
                    for n in range(4):
                        un[m, h * nz + 4 * g + n, ch] = blocks[n].astype(BF16)
            return 0

        lax.fori_loop(0, nz, step, 0)

        def send(t, _):
            p = lax.rem(mine + 1 + t, nq)

            @pl.when(p == mine)
            def _():
                pltpu.make_async_copy(un.at[m, p], out.at[m, mine], r4.at[m]).start()

            @pl.when(p != mine)
            def _():
                pltpu.make_async_remote_copy(
                    src_ref=un.at[m, p],
                    dst_ref=out.at[m, mine],
                    send_sem=s4,
                    recv_sem=r4.at[m],
                    device_id=(2 * z + p // nz, 2 * (p % nz) + core),
                    device_id_type=MESH,
                ).start()

            return 0

        lax.fori_loop(0, nq, send, 0)

    for m in range(nch):
        wait_all(za.at[m], r2a.at[m])
        swap(m).start()
        multiply(za.at[m], m, core)
        swap(m).wait_recv()
        multiply(other.at[m], m, 1 - core)
        send_products(m)
        if m:
            split_and_send(m - 1)
    split_and_send(nch - 1)
    for m in range(nch):
        wait_all(out.at[m], r4.at[m])

    for arr in range(2):
        for m in range(nch):

            @pl.when(core == yl)
            def _():
                wait_all(ab.at[arr, m, 0 : nq - 1], s1)

            @pl.when(core != yl)
            def _():
                wait_all(ab.at[arr, m], s1)

            wait_all(zs.at[arr, m, 0 : nz - 1], s2)
    for m in range(nch):
        swap(m).wait_send()
        wait_all(prods.at[m, 0 : nz - 1], s3)
        wait_all(un.at[m, 0 : nq - 1], s4)


def exchange(ab, nz):
    _, nch, nq, _, ci, _ = ab.shape
    ti = nch * ci
    depth = nq * ti
    sem = pltpu.SemaphoreType.DMA
    vmem = pl.BlockSpec(memory_space=pltpu.VMEM)
    return pl.pallas_call(
        functools.partial(triangle_kernel, nz, nch, ci),
        out_shape=jax.ShapeDtypeStruct((nch, nq, nz, ci, LANES), BF16),
        in_specs=[vmem],
        out_specs=vmem,
        scratch_shapes=[
            pltpu.VMEM((2, nch, nq, nz, ci, LANES), BF16),
            pltpu.VMEM((2, nch, nz, ci, depth), BF16),
            pltpu.VMEM((nch, nz, ci, depth), BF16),
            pltpu.VMEM((nz, ti, depth), BF16),
            pltpu.VMEM((nch, nz, ci, depth), BF16),
            pltpu.VMEM((nch, nz, 2, nz // 4, ci, 4 * ti), BF16),
            pltpu.VMEM((nch, nz, 2, nz // 4, ci, 4 * ti), BF16),
            pltpu.VMEM((nch, nq, nz, ci, LANES), BF16),
            sem,
            sem((2, nch)),
            sem,
            sem((nch,)),
            sem,
            sem((nch,)),
            sem((nch,)),
            sem,
            sem((nch,)),
            sem,
            sem((nch,)),
        ],
        compiler_params=pltpu.CompilerParams(
            collective_id=0, has_side_effects=True, vmem_limit_bytes=56 * 2**20
        ),
    )(ab)


def local(pair, residue_mask, norm_gain, w_in, b_in, w_gate, b_gate, out_gain, w_out, b_out):
    ti, tj, _ = pair.shape
    channels = w_in.shape[1] // 4
    nz = lax.axis_size("row") // 2
    nq = 2 * nz
    ci = 32
    nch = ti // ci
    row_index = lax.axis_index("row")
    col_index = lax.axis_index("col")
    valid = residue_mask.astype(F32)
    row_mask = lax.dynamic_slice_in_dim(valid, row_index * ti, ti)
    col_mask = lax.dynamic_slice_in_dim(valid, col_index * tj, tj)
    source = pair.astype(F32)
    mean = jnp.mean(source, axis=-1, keepdims=True)
    centred = source - mean
    var = jnp.mean(centred * centred, axis=-1, keepdims=True)
    normed = (centred * lax.rsqrt(var + 1e-05) * norm_gain).astype(BF16)
    proj = (
        jnp.einsum("ijd,de->eij", normed, w_in, preferred_element_type=F32) + b_in[:, None, None]
    )
    masked = row_mask[:, None] * col_mask[None, :]
    a_tile = masked * jax.nn.sigmoid(proj[channels : 2 * channels]) * proj[:channels]
    b_tile = masked * jax.nn.sigmoid(proj[3 * channels :]) * proj[2 * channels : 3 * channels]
    ab = jnp.stack([a_tile, b_tile]).astype(BF16)
    ab = jnp.pad(ab, ((0, 0), (0, 0), (0, 0), (0, LANES - tj)))
    ab = ab.reshape(2, nq, nz, nch, ci, LANES).transpose(0, 3, 1, 2, 4, 5)
    moved = exchange(ab, nz)
    prod = moved.transpose(1, 2, 0, 3, 4).reshape(channels, ti, LANES)[:, :, :tj].astype(F32)
    prod_mean = jnp.mean(prod, axis=0, keepdims=True)
    prod_centred = prod - prod_mean
    prod_var = jnp.mean(prod_centred * prod_centred, axis=0, keepdims=True)
    prod_norm = (prod_centred * lax.rsqrt(prod_var + 1e-05) * out_gain[:, None, None]).astype(BF16)
    linear = jnp.einsum("cij,ce->ije", prod_norm, w_out, preferred_element_type=F32) + b_out
    gating = jax.nn.sigmoid(
        jnp.einsum("ijd,de->ije", normed, w_gate, preferred_element_type=F32) + b_gate
    )
    return (gating * linear).astype(BF16)


def solution(mesh):
    in_specs = (P("row", "col", None), P(), P(), P(), P(), P(), P(), P(), P(), P())
    out_specs = P("row", "col", None)
    return jax.shard_map(local, mesh=mesh, in_specs=in_specs, out_specs=out_specs, check_vma=False)
```

```python
import functools

import jax
import jax.numpy as jnp
from jax import lax
from jax.experimental import pallas as pl
from jax.experimental.pallas import tpu as pltpu
from jax.sharding import PartitionSpec as P

MESH = pl.DeviceIdType.MESH
BF16 = jnp.bfloat16
F32 = jnp.float32
LANES = 128
CHUNK = 32


def join4(parts):
    lane = lax.broadcasted_iota(jnp.int32, parts[0].shape, 1)
    one, two, three = (pltpu.roll(parts[n], 128 - 32 * n, 1) for n in (1, 2, 3))
    return (
        jnp.where(lane < 96, parts[0], one),
        jnp.where(lane < 64, one, two),
        jnp.where(lane < 32, two, three),
    )


def split4(parts):
    lane = lax.broadcasted_iota(jnp.int32, parts[0].shape, 1)
    first, second, third = parts
    return (
        first,
        jnp.where(lane < 32, pltpu.roll(first, 32, 1), pltpu.roll(second, 32, 1)),
        jnp.where(lane < 64, pltpu.roll(second, 64, 1), pltpu.roll(third, 64, 1)),
        pltpu.roll(third, 96, 1),
    )


def sigmoid(x):
    return 0.5 * jnp.tanh(0.5 * x) + 0.5


def triangle_kernel(
    nz,
    nch,
    ci,
    pair,
    mask,
    norm_gain,
    w_in,
    b_in,
    w_gate,
    b_gate,
    out_gain,
    w_out,
    b_out,
    update,
    nrm,
    wt,
    bias,
    gate,
    flip,
    ab,
    recv1,
    zs,
    za,
    zb,
    other,
    prods,
    back,
    un,
    land,
    s1,
    r1,
    s2,
    r2a,
    r2b,
    so,
    ro,
    s3,
    r3,
    s4,
    r4,
):
    nq = 2 * nz
    row, col = lax.axis_index("row"), lax.axis_index("col")
    z, yl = row // 2, row % 2
    w, core = col // 2, col % 2
    mine = yl * nz + w

    barrier = pltpu.get_barrier_semaphore()

    def greet_plane(t, _):
        dev = lax.rem(yl * nq + col + t, 2 * nq)
        pl.semaphore_signal(
            barrier, inc=1, device_id=(2 * z + dev // nq, dev % nq), device_id_type=MESH
        )
        return 0

    lax.fori_loop(1, 2 * nq, greet_plane, 0)

    def greet_line(t, _):
        pl.semaphore_signal(
            barrier, inc=1, device_id=(2 * lax.rem(z + t, nz) + yl, col), device_id_type=MESH
        )
        return 0

    lax.fori_loop(1, nz, greet_line, 0)

    channels = nq * nz
    ti, tj, cz = pair.shape

    turned = w_in[...].astype(F32).T.astype(BF16)
    column = jnp.broadcast_to(b_in[...], (LANES, 4 * channels)).T
    for arr in range(2):
        wt[arr] = turned[2 * arr * channels : 2 * (arr + 1) * channels]
        bias[arr] = column[2 * arr * channels : 2 * (arr + 1) * channels]
    nrm[:, tj:, :] = jnp.zeros((ti, LANES - tj, cz), BF16)

    def front(arr, m):
        def step(q, _):
            i0 = m * ci + 4 * q
            if arr == 1:
                x = pair[pl.ds(i0, 4)].astype(F32)
                centred = x - jnp.mean(x, axis=-1, keepdims=True)
                var = jnp.mean(centred * centred, axis=-1, keepdims=True)
                y = centred * lax.rsqrt(var + 1e-05) * norm_gain[...].reshape(1, 1, cz)
                nrm[pl.ds(i0, 4), 0:tj, :] = y.astype(BF16)
            rhs = nrm[pl.ds(i0, 4)].reshape(4 * LANES, cz)
            res = lax.dot_general(
                wt[arr], rhs, (((1,), (1,)), ((), ())), preferred_element_type=F32
            )
            for t in range(4):
                value = res[0:channels, t * LANES : (t + 1) * LANES] + bias[arr, 0:channels]
                gating = res[channels:, t * LANES : (t + 1) * LANES] + bias[arr, channels:]
                flip[pl.ds(4 * q + t, channels, stride=ci), :] = (
                    mask[pl.ds(i0 + t, 1), :] * sigmoid(gating) * value
                )
            return 0

        lax.fori_loop(0, ci // 4, step, 0)

        def pack(p, _):
            for ch in range(nz):
                ab[arr, m, p, ch] = flip[
                    pl.ds(pl.multiple_of((p * nz + ch) * ci, ci), ci), :
                ].astype(BF16)
            return 0

        lax.fori_loop(0, nq, pack, 0)

    def gates(q, _):
        rows = nrm[pl.ds(4 * q, 4)].reshape(4 * LANES, cz)
        res = jnp.dot(rows, w_gate[...], preferred_element_type=F32) + b_gate[...]
        gate[pl.ds(4 * q, 4)] = sigmoid(res).reshape(4, LANES, cz)[:, 0:tj]
        return 0

    def finish(m):
        wait_all(land.at[m], r4.at[m])

        def add(p, total):
            for ch in range(nz):
                total = total + land[m, p, ch].astype(F32)
            return total

        zero = jnp.zeros((ci, LANES), F32)
        mean = lax.fori_loop(0, nq, add, zero) * (1.0 / channels)

        def add_square(p, total):
            for ch in range(nz):
                centred = land[m, p, ch].astype(F32) - mean
                total = total + centred * centred
            return total

        var = lax.fori_loop(0, nq, add_square, zero) * (1.0 / channels)
        scale = lax.rsqrt(var + 1e-05)

        def scaled(p, _):
            for ch in range(nz):
                c = p * nz + ch
                flip[pl.ds(pl.multiple_of(c * ci, ci), ci), :] = (
                    (land[m, p, ch].astype(F32) - mean) * scale * out_gain[0, c]
                )
            return 0

        lax.fori_loop(0, nq, scaled, 0)

        def emit(i, _):
            normal = flip[pl.ds(i, channels, stride=ci), :].astype(BF16)
            linear = lax.dot_general(
                normal, w_out[...], (((0,), (0,)), ((), ())), preferred_element_type=F32
            )
            update[m * ci + i] = ((linear[0:tj] + b_out[...]) * gate[m * ci + i]).astype(BF16)
            return 0

        lax.fori_loop(0, ci, emit, 0)

    def send1(arr, m):
        def step(t, _):
            p = lax.rem(mine + t, nq)
            here = jnp.logical_and(p == mine, core == yl)

            @pl.when(here)
            def _():
                pltpu.make_async_copy(ab.at[arr, m, p], recv1.at[arr, m, col], r1.at[arr, m]).start()

            @pl.when(jnp.logical_not(here))
            def _():
                pltpu.make_async_remote_copy(
                    src_ref=ab.at[arr, m, p],
                    dst_ref=recv1.at[arr, m, col],
                    send_sem=s1,
                    recv_sem=r1.at[arr, m],
                    device_id=(2 * z + p // nz, 2 * (p % nz) + yl),
                    device_id_type=MESH,
                ).start()

            return 0

        lax.fori_loop(0, nq, step, 0)

    def wait_all(ref, sem):
        pltpu.make_async_copy(ref, ref, sem).wait()

    def send_line(src, dst, target, send_sem, recv_sem):
        @pl.when(target == z)
        def _():
            pltpu.make_async_copy(src, dst, recv_sem).start()

        @pl.when(target != z)
        def _():
            pltpu.make_async_remote_copy(
                src_ref=src,
                dst_ref=dst,
                send_sem=send_sem,
                recv_sem=recv_sem,
                device_id=(2 * target + yl, col),
                device_id_type=MESH,
            ).start()

    def join_and_send(arr, m):
        def step(t, _):
            ch = lax.rem(z + 1 + t, nz)
            for g in range(nq // 4):
                blocks = join4([recv1[arr, m, 4 * g + n, ch].astype(F32) for n in range(4)])
                for n in range(3):
                    zs[arr, m, ch, :, (3 * g + n) * LANES : (3 * g + n + 1) * LANES] = blocks[
                        n
                    ].astype(BF16)
            if arr == 0:
                send_line(zs.at[0, m, ch], za.at[m, z], ch, s2, r2a.at[m])
            else:
                send_line(zs.at[1, m, ch], zb.at[z, m * ci : (m + 1) * ci], ch, s2, r2b)
            return 0

        lax.fori_loop(0, nz, step, 0)

    order = [(1, m) for m in range(nch)] + [(0, m) for m in range(nch)]
    front(*order[0])
    pl.semaphore_wait(barrier, 2 * nq - 1 + nz - 1)
    send1(*order[0])
    front(*order[1])
    send1(*order[1])
    for n, (arr, m) in enumerate(order):
        wait_all(recv1.at[arr, m], r1.at[arr, m])
        join_and_send(arr, m)
        if n + 2 < len(order):
            front(*order[n + 2])
            send1(*order[n + 2])

    lax.fori_loop(0, ti // 4, gates, 0)
    wait_all(zb, r2b)

    def multiply(lhs_ref, m, h):
        lhs = lhs_ref[...].reshape(nz * ci, lhs_ref.shape[-1])

        def step(g, _):
            rhs = zb[pl.ds(4 * g, 4)].reshape(4 * ti, zb.shape[-1])
            res = lax.dot_general(lhs, rhs, (((1,), (1,)), ((), ())), preferred_element_type=F32)
            prods[m, :, h, g] = res.reshape(nz, ci, 4 * ti).astype(BF16)
            return 0

        lax.fori_loop(0, nz // 4, step, 0)

    def swap(m):
        return pltpu.make_async_remote_copy(
            src_ref=za.at[m],
            dst_ref=other.at[m],
            send_sem=so.at[m],
            recv_sem=ro.at[m],
            device_id=(row, 2 * w + 1 - core),
            device_id_type=MESH,
        )

    def send_products(m):
        def step(t, _):
            target = lax.rem(z + 1 + t, nz)
            send_line(prods.at[m, target], back.at[m, z], target, s3, r3.at[m])
            return 0

        lax.fori_loop(0, nz, step, 0)

    def split_and_send(m):
        wait_all(back.at[m], r3.at[m])

        def step(ch, _):
            for h in range(2):
                for g in range(nz // 4):
                    blocks = split4(
                        [
                            back[m, ch, h, g, :, n * LANES : (n + 1) * LANES].astype(F32)
                            for n in range(3)
                        ]
                    )
                    for n in range(4):
                        un[m, h * nz + 4 * g + n, ch] = blocks[n].astype(BF16)
            return 0

        lax.fori_loop(0, nz, step, 0)

        def send(t, _):
            p = lax.rem(mine + 1 + t, nq)

            @pl.when(p == mine)
            def _():
                pltpu.make_async_copy(un.at[m, p], land.at[m, mine], r4.at[m]).start()

            @pl.when(p != mine)
            def _():
                pltpu.make_async_remote_copy(
                    src_ref=un.at[m, p],
                    dst_ref=land.at[m, mine],
                    send_sem=s4,
                    recv_sem=r4.at[m],
                    device_id=(2 * z + p // nz, 2 * (p % nz) + core),
                    device_id_type=MESH,
                ).start()

            return 0

        lax.fori_loop(0, nq, send, 0)

    for m in range(nch):
        wait_all(za.at[m], r2a.at[m])
        swap(m).start()
        multiply(za.at[m], m, core)
        swap(m).wait_recv()
        multiply(other.at[m], m, 1 - core)
        send_products(m)
        if m:
            split_and_send(m - 1)
        if m > 1:
            finish(m - 2)
    split_and_send(nch - 1)
    finish(nch - 2)
    finish(nch - 1)

    for arr in range(2):
        for m in range(nch):

            @pl.when(core == yl)
            def _():
                wait_all(ab.at[arr, m, 0 : nq - 1], s1)

            @pl.when(core != yl)
            def _():
                wait_all(ab.at[arr, m], s1)

            wait_all(zs.at[arr, m, 0 : nz - 1], s2)
    for m in range(nch):
        swap(m).wait_send()
        wait_all(prods.at[m, 0 : nz - 1], s3)
        wait_all(un.at[m, 0 : nq - 1], s4)


def local(pair, residue_mask, norm_gain, w_in, b_in, w_gate, b_gate, out_gain, w_out, b_out):
    ti, tj, cz = pair.shape
    channels = w_in.shape[1] // 4
    nz = lax.axis_size("row") // 2
    nq = 2 * nz
    ci = CHUNK
    nch = ti // ci
    depth = nq * ti
    valid = residue_mask.astype(F32)
    row_mask = lax.dynamic_slice_in_dim(valid, lax.axis_index("row") * ti, ti)
    col_mask = lax.dynamic_slice_in_dim(valid, lax.axis_index("col") * tj, tj)
    mask = row_mask[:, None] * jnp.pad(col_mask, (0, LANES - tj))[None, :]
    sem = pltpu.SemaphoreType.DMA
    vmem = pl.BlockSpec(memory_space=pltpu.VMEM)
    smem = pl.BlockSpec(memory_space=pltpu.SMEM)
    return pl.pallas_call(
        functools.partial(triangle_kernel, nz, nch, ci),
        out_shape=jax.ShapeDtypeStruct((ti, tj, cz), BF16),
        in_specs=[vmem] * 7 + [smem] + [vmem] * 2,
        out_specs=vmem,
        scratch_shapes=[
            pltpu.VMEM((ti, LANES, cz), BF16),
            pltpu.VMEM((2, 2 * channels, cz), BF16),
            pltpu.VMEM((2, 2 * channels, LANES), F32),
            pltpu.VMEM((ti, tj, cz), F32),
            pltpu.VMEM((channels * ci, LANES), F32),
            pltpu.VMEM((2, nch, nq, nz, ci, LANES), BF16),
            pltpu.VMEM((2, nch, nq, nz, ci, LANES), BF16),
            pltpu.VMEM((2, nch, nz, ci, depth), BF16),
            pltpu.VMEM((nch, nz, ci, depth), BF16),
            pltpu.VMEM((nz, ti, depth), BF16),
            pltpu.VMEM((nch, nz, ci, depth), BF16),
            pltpu.VMEM((nch, nz, 2, nz // 4, ci, 4 * ti), BF16),
            pltpu.VMEM((nch, nz, 2, nz // 4, ci, 4 * ti), BF16),
            pltpu.VMEM((nch, nq, nz, ci, LANES), BF16),
            pltpu.VMEM((nch, nq, nz, ci, LANES), BF16),
            sem,
            sem((2, nch)),
            sem,
            sem((nch,)),
            sem,
            sem((nch,)),
            sem((nch,)),
            sem,
            sem((nch,)),
            sem,
            sem((nch,)),
        ],
        compiler_params=pltpu.CompilerParams(
            collective_id=0, has_side_effects=True, vmem_limit_bytes=60 * 2**20
        ),
    )(
        pair,
        mask,
        norm_gain.reshape(1, cz),
        w_in,
        b_in.reshape(1, 4 * channels),
        w_gate,
        b_gate.reshape(1, cz),
        out_gain.reshape(1, channels),
        w_out,
        b_out.reshape(1, cz),
    )


def solution(mesh):
    in_specs = (P("row", "col", None), P(), P(), P(), P(), P(), P(), P(), P(), P())
    out_specs = P("row", "col", None)
    return jax.shard_map(local, mesh=mesh, in_specs=in_specs, out_specs=out_specs, check_vma=False)
```

```python
import functools

import jax
import jax.numpy as jnp
from jax import lax
from jax.experimental import pallas as pl
from jax.experimental.pallas import tpu as pltpu
from jax.sharding import PartitionSpec as P

MESH = pl.DeviceIdType.MESH
BF16 = jnp.bfloat16
F32 = jnp.float32
LANES = 128
CHUNK = 16
SITES = 4


def sigmoid(x):
    return 0.5 * jnp.tanh(0.5 * x) + 0.5


def join4(parts):
    lane = lax.broadcasted_iota(jnp.int32, parts[0].shape, 1)
    one, two, three = (pltpu.roll(parts[n], 128 - 32 * n, 1) for n in (1, 2, 3))
    return (
        jnp.where(lane < 96, parts[0], one),
        jnp.where(lane < 64, one, two),
        jnp.where(lane < 32, two, three),
    )


def turn8(parts):
    slot = lax.broadcasted_iota(jnp.int32, parts[0].shape, 1) // 16
    for step in (1, 2, 4):
        low = (slot // step) % 2 == 0
        turned = list(parts)
        for i in range(8):
            if not i & step:
                first, second = parts[i], parts[i | step]
                turned[i] = jnp.where(low, first, pltpu.roll(second, 16 * step, 1))
                turned[i | step] = jnp.where(low, pltpu.roll(first, 128 - 16 * step, 1), second)
        parts = turned
    return parts


def over_slots(x):
    for step in (16, 32, 64):
        x = x + pltpu.roll(x, step, 1)
    return x


def triangle_kernel(
    nz,
    pair,
    mask,
    norm_gain,
    w_in,
    b_in,
    w_gate,
    b_gate,
    out_gain,
    w_out,
    b_out,
    update,
    nrm,
    wt,
    bias,
    gate,
    flip,
    flop,
    ab,
    recv1,
    zs,
    za,
    zb,
    prods,
    back,
    un,
    land,
    s1,
    r1,
    s2,
    r2a,
    r2b,
    sf,
    rf,
    so,
    ro,
    s3,
    r3,
    s4,
    r4,
):
    nq = 2 * nz
    ci = CHUNK
    channels = nq * nz
    ti, tj, cz = pair.shape
    nch = ti // ci
    row, col = lax.axis_index("row"), lax.axis_index("col")
    z, yl = row // 2, row % 2
    w, core = col // 2, col % 2
    mine = yl * nz + w

    ahead = (nz - SITES) // 2
    site_of = [min(max(place - ahead, 0), SITES - 1) for place in range(nz)]
    group = [(site_of.index(e), site_of.index(e) + site_of.count(e)) for e in range(SITES)]
    shift = [site_of[place] - place + ahead for place in range(nz)]
    n_remote = sum(1 for d in shift if d)

    def along(d):
        return (2 * lax.rem(z + (d + nz) % nz, nz) + yl, col)

    barrier = pltpu.get_barrier_semaphore()

    def greet_plane(t, _):
        dev = lax.rem(yl * nq + col + t, 2 * nq)
        pl.semaphore_signal(
            barrier, inc=1, device_id=(2 * z + dev // nq, dev % nq), device_id_type=MESH
        )
        return 0

    lax.fori_loop(1, 2 * nq, greet_plane, 0)
    for d in range(1, ahead + 1):
        for sign in (1, -1):
            pl.semaphore_signal(barrier, inc=1, device_id=along(sign * d), device_id_type=MESH)

    turned = w_in[...].astype(F32).T.astype(BF16)
    column = jnp.broadcast_to(b_in[...], (LANES, 4 * channels)).T
    for arr in range(2):
        wt[arr] = turned[2 * arr * channels : 2 * (arr + 1) * channels]
        bias[arr] = column[2 * arr * channels : 2 * (arr + 1) * channels]
    nrm[:, tj:, :] = jnp.zeros((ti, LANES - tj, cz), BF16)
    normed = set()

    def front(arr, m):
        fresh = m not in normed
        normed.add(m)

        def step(q, _):
            i0 = m * ci + 4 * q
            if fresh:
                x = pair[pl.ds(i0, 4)].astype(F32)
                centred = x - jnp.mean(x, axis=-1, keepdims=True)
                var = jnp.mean(centred * centred, axis=-1, keepdims=True)
                y = centred * lax.rsqrt(var + 1e-05) * norm_gain[...].reshape(1, 1, cz)
                nrm[pl.ds(i0, 4), 0:tj, :] = y.astype(BF16)
            rhs = nrm[pl.ds(i0, 4)].reshape(4 * LANES, cz)
            res = lax.dot_general(
                wt[arr], rhs, (((1,), (1,)), ((), ())), preferred_element_type=F32
            )
            for t in range(4):
                value = res[0:channels, t * LANES : (t + 1) * LANES] + bias[arr, 0:channels]
                gating = res[channels:, t * LANES : (t + 1) * LANES] + bias[arr, channels:]
                flip[pl.ds(4 * q + t, channels, stride=ci), :] = (
                    mask[pl.ds(i0 + t, 1), :] * sigmoid(gating) * value
                )
            return 0

        lax.fori_loop(0, ci // 4, step, 0)

        def pack(p, _):
            for ch in range(nz):
                ab[arr, m, p, ch] = flip[
                    pl.ds(pl.multiple_of((p * nz + ch) * ci, ci), ci), :
                ].astype(BF16)
            return 0

        lax.fori_loop(0, nq, pack, 0)

    def gates(q, _):
        rows = nrm[pl.ds(4 * q, 4)].reshape(4 * LANES, cz)
        res = jnp.dot(rows, w_gate[...], preferred_element_type=F32) + b_gate[...]
        gate[pl.ds(4 * q, 4)] = sigmoid(res).reshape(4, LANES, cz)[:, 0:tj]
        return 0

    def wait_all(ref, sem):
        pltpu.make_async_copy(ref, ref, sem).wait()

    def send(src, dst, send_sem, recv_sem, device):
        pltpu.make_async_remote_copy(
            src_ref=src,
            dst_ref=dst,
            send_sem=send_sem,
            recv_sem=recv_sem,
            device_id=device,
            device_id_type=MESH,
        ).start()

    def send1(arr, m):
        def step(t, _):
            p = lax.rem(mine + t, nq)
            here = jnp.logical_and(p == mine, core == yl)

            @pl.when(here)
            def _():
                pltpu.make_async_copy(ab.at[arr, m, p], recv1.at[arr, m, col], r1.at[arr, m]).start()

            @pl.when(jnp.logical_not(here))
            def _():
                send(
                    ab.at[arr, m, p],
                    recv1.at[arr, m, col],
                    s1,
                    r1.at[arr, m],
                    (2 * z + p // nz, 2 * (p % nz) + yl),
                )

            return 0

        lax.fori_loop(0, nq, step, 0)

    def enter(arr, m):
        wait_all(recv1.at[arr, m], r1.at[arr, m])

        def step(place, _):
            ch = lax.rem(z - place + ahead + nz, nz)
            for g in range(nq // 4):
                blocks = join4([recv1[arr, m, 4 * g + n, ch].astype(F32) for n in range(4)])
                for n in range(3):
                    zs[arr, m, place, :, (3 * g + n) * LANES : (3 * g + n + 1) * LANES] = blocks[
                        n
                    ].astype(BF16)
            return 0

        lax.fori_loop(0, nz, step, 0)
        for place in sorted(range(nz), key=lambda n: -abs(shift[n])):
            if arr == 0:
                dst = za.at[core, place, m * ci : (m + 1) * ci]
                sem = r2a.at[m]
            else:
                dst = zb.at[site_of[place], m, place]
                sem = r2b.at[m, site_of[place]]
            if shift[place]:
                send(zs.at[arr, m, place], dst, s2, sem, along(shift[place]))
            else:
                pltpu.make_async_copy(zs.at[arr, m, place], dst, sem).start()

    def held(site, m, e):
        return zb.at[site, m, group[e][0] : group[e][1]]

    passed = []

    def pass_on(m, s):
        for site in range(SITES):
            if s == 1:
                wait_all(held(site, m, site), r2b.at[m, site])
            for way, e, to in ((0, site - s + 1, site + 1), (1, site + s - 1, site - 1)):
                if 0 <= e < SITES and 0 <= to < SITES:
                    if s > 1:
                        wait_all(held(site, m, e), rf.at[m, s - 1, site, way])
                    send(
                        held(site, m, e),
                        held(to, m, e),
                        sf,
                        rf.at[m, s, to, way],
                        along(to - site),
                    )
                    passed.append((site, m, e))

    def swap(m):
        part = za.at[core, :, m * ci : (m + 1) * ci]
        return pltpu.make_async_remote_copy(
            src_ref=part,
            dst_ref=part,
            send_sem=so.at[m],
            recv_sem=ro.at[m],
            device_id=(row, 2 * w + 1 - core),
            device_id_type=MESH,
        )

    def product(m):
        for s in range(1, SITES):
            wait_all(held(SITES - 1, m, SITES - 1 - s), rf.at[m, s, SITES - 1, 0])
            wait_all(held(0, m, s), rf.at[m, s, 0, 1])
        for site in range(SITES):
            first, last = group[site]

            def step(h, _):
                lhs = za[h, first:last].reshape((last - first) * ti, za.shape[-1])
                rhs = zb[site, m].reshape(nz * ci, zb.shape[-1])
                res = lax.dot_general(
                    lhs, rhs, (((1,), (1,)), ((), ())), preferred_element_type=F32
                )
                prods[m, first:last, h] = res.reshape(last - first, ti, nz * ci).astype(BF16)
                return 0

            lax.fori_loop(0, 2, step, 0)
        for place in sorted(range(nz), key=lambda n: -abs(shift[n])):
            dst = back.at[m, lax.rem(z - site_of[place] + nz, nz)]
            if shift[place]:
                send(prods.at[m, place], dst, s3, r3.at[m], along(-shift[place]))
            else:
                pltpu.make_async_copy(prods.at[m, place], dst, r3.at[m]).start()

    def turn_and_send(m):
        wait_all(back.at[m], r3.at[m])

        def step(n, _):
            h, rows = n // (ti // 16), pl.ds(pl.multiple_of(n % (ti // 16) * 16, 16), 16)
            blocks = [
                pltpu.roll(back[m, ch, h, rows].astype(F32), 16 * ((ch - ahead) % 8), 1)
                if ch != ahead
                else back[m, ch, h, rows].astype(F32)
                for ch in range(nz)
            ]
            for n, block in enumerate(turn8(blocks)):
                un[m, h * nz + n, rows] = block.astype(BF16)
            return 0

        lax.fori_loop(0, 2 * (ti // 16), step, 0)

        def go(t, _):
            p = lax.rem(mine + 1 + t, nq)

            @pl.when(p == mine)
            def _():
                pltpu.make_async_copy(un.at[m, p], land.at[m, mine], r4.at[m]).start()

            @pl.when(p != mine)
            def _():
                send(
                    un.at[m, p],
                    land.at[m, mine],
                    s4,
                    r4.at[m],
                    (2 * z + p // nz, 2 * (p % nz) + core),
                )

            return 0

        lax.fori_loop(0, nq, go, 0)

    def finish(m):
        wait_all(land.at[m], r4.at[m])
        zero = jnp.zeros((ti, LANES), F32)

        def add(p, total):
            return total + land[m, p].astype(F32)

        mean = over_slots(lax.fori_loop(0, nq, add, zero)) * (1.0 / channels)

        def add_square(p, total):
            centred = land[m, p].astype(F32) - mean
            return total + centred * centred

        var = over_slots(lax.fori_loop(0, nq, add_square, zero)) * (1.0 / channels)
        scale = lax.rsqrt(var + 1e-05)

        def scaled(p, _):
            y = (land[m, p].astype(F32) - mean) * scale * out_gain[pl.ds(p, 1), :]
            y = jnp.concatenate([y, jnp.zeros((LANES - ti, LANES), F32)], axis=0)
            flip[pl.ds(pl.multiple_of(p * LANES, LANES), LANES), :] = y.T
            return 0

        lax.fori_loop(0, nq, scaled, 0)

        def mix(j, _):
            normal = flip[pl.ds(j, channels, stride=ci), :].astype(BF16)
            linear = lax.dot_general(
                normal, w_out[...], (((0,), (0,)), ((), ())), preferred_element_type=F32
            )
            flop[pl.ds(j, ti, stride=ci), :] = linear[0:ti]
            return 0

        lax.fori_loop(0, ci, mix, 0)

        def emit(i, _):
            linear = flop[pl.ds(pl.multiple_of(i * ci, ci), ci), :] + b_out[...]
            columns = slice(m * ci, (m + 1) * ci)
            update[i, columns, :] = (linear * gate[i, columns, :]).astype(BF16)
            return 0

        lax.fori_loop(0, ti, emit, 0)

    order, b_next, a_next = [], 0, 0
    while b_next < nch:
        order.append((1, b_next))
        b_next += 1
        for _ in range(2):
            if a_next < nch:
                order.append((0, a_next))
                a_next += 1

    front(*order[0])
    pl.semaphore_wait(barrier, 2 * nq - 1 + 2 * ahead)
    send1(*order[0])
    front(*order[1])
    send1(*order[1])

    def later(k):
        for s in range(1, SITES):
            if 0 <= k - s < nch:
                pass_on(k - s, s)
        if k == SITES:
            for m in range(nch):
                swap(m).wait_recv()
        if 0 <= k - SITES < nch:
            product(k - SITES)
        if 0 <= k - SITES - 1 < nch:
            turn_and_send(k - SITES - 1)
        if 0 <= k - SITES - 2 < nch:
            finish(k - SITES - 2)

    for n, (arr, m) in enumerate(order):
        enter(arr, m)
        if n + 2 < len(order):
            front(*order[n + 2])
            send1(*order[n + 2])
        if arr == 1:
            later(m)
        elif m:
            wait_all(za.at[core, :, (m - 1) * ci : m * ci], r2a.at[m - 1])
            swap(m - 1).start()
        if (arr, m) == (0, nch - 1):
            lax.fori_loop(0, ti // 4, gates, 0)
            wait_all(za.at[core, :, m * ci :], r2a.at[m])
            swap(m).start()
    for k in range(nch, nch + SITES + 2):
        later(k)

    for arr in range(2):
        for m in range(nch):

            @pl.when(core == yl)
            def _():
                wait_all(ab.at[arr, m, 0 : nq - 1], s1)

            @pl.when(core != yl)
            def _():
                wait_all(ab.at[arr, m], s1)

            wait_all(zs.at[arr, m, 0:n_remote], s2)
    for site, m, e in passed:
        wait_all(held(site, m, e), sf)
    for m in range(nch):
        swap(m).wait_send()
        wait_all(prods.at[m, 0:n_remote], s3)
        wait_all(un.at[m, 0 : nq - 1], s4)


def local(pair, residue_mask, norm_gain, w_in, b_in, w_gate, b_gate, out_gain, w_out, b_out):
    ti, tj, cz = pair.shape
    channels = w_in.shape[1] // 4
    nz = lax.axis_size("row") // 2
    nq = 2 * nz
    ci = CHUNK
    nch = ti // ci
    depth = nq * ti
    valid = residue_mask.astype(F32)
    row_mask = lax.dynamic_slice_in_dim(valid, lax.axis_index("row") * ti, ti)
    col_mask = lax.dynamic_slice_in_dim(valid, lax.axis_index("col") * tj, tj)
    mask = row_mask[:, None] * jnp.pad(col_mask, (0, LANES - tj))[None, :]
    sem = pltpu.SemaphoreType.DMA
    vmem = pl.BlockSpec(memory_space=pltpu.VMEM)
    return pl.pallas_call(
        functools.partial(triangle_kernel, nz),
        out_shape=jax.ShapeDtypeStruct((ti, tj, cz), BF16),
        in_specs=[vmem] * 10,
        out_specs=vmem,
        scratch_shapes=[
            pltpu.VMEM((ti, LANES, cz), BF16),
            pltpu.VMEM((2, 2 * channels, cz), BF16),
            pltpu.VMEM((2, 2 * channels, LANES), F32),
            pltpu.VMEM((ti, tj, cz), F32),
            pltpu.VMEM((channels * ci, LANES), F32),
            pltpu.VMEM((ti * ci, cz), F32),
            pltpu.VMEM((2, nch, nq, nz, ci, LANES), BF16),
            pltpu.VMEM((2, nch, nq, nz, ci, LANES), BF16),
            pltpu.VMEM((2, nch, nz, ci, depth), BF16),
            pltpu.VMEM((2, nz, ti, depth), BF16),
            pltpu.VMEM((SITES, nch, nz, ci, depth), BF16),
            pltpu.VMEM((nch, nz, 2, ti, nz * ci), BF16),
            pltpu.VMEM((nch, nz, 2, ti, nz * ci), BF16),
            pltpu.VMEM((nch, nq, ti, LANES), BF16),
            pltpu.VMEM((nch, nq, ti, LANES), BF16),
            sem,
            sem((2, nch)),
            sem,
            sem((nch,)),
            sem((nch, SITES)),
            sem,
            sem((nch, SITES, SITES, 2)),
            sem((nch,)),
            sem((nch,)),
            sem,
            sem((nch,)),
            sem,
            sem((nch,)),
        ],
        compiler_params=pltpu.CompilerParams(
            collective_id=0, has_side_effects=True, vmem_limit_bytes=60 * 2**20
        ),
    )(
        pair,
        mask,
        norm_gain.reshape(1, cz),
        w_in,
        b_in.reshape(1, 4 * channels),
        w_gate,
        b_gate.reshape(1, cz),
        jnp.repeat(out_gain, ci).reshape(nq, LANES),
        w_out,
        b_out.reshape(1, cz),
    )


def solution(mesh):
    in_specs = (P("row", "col", None), P(), P(), P(), P(), P(), P(), P(), P(), P())
    out_specs = P("row", "col", None)
    return jax.shard_map(local, mesh=mesh, in_specs=in_specs, out_specs=out_specs, check_vma=False)
```

```python
import functools

import jax
import jax.numpy as jnp
from jax import lax
from jax.experimental import pallas as pl
from jax.experimental.pallas import tpu as pltpu
from jax.sharding import PartitionSpec as P

MESH = pl.DeviceIdType.MESH
BF16 = jnp.bfloat16
F32 = jnp.float32
LANES = 128
CHUNK = 16
SITES = 2


def sigmoid(x):
    return 0.5 * jnp.tanh(0.5 * x) + 0.5


def join4(parts):
    lane = lax.broadcasted_iota(jnp.int32, parts[0].shape, 1)
    one, two, three = (pltpu.roll(parts[n], 128 - 32 * n, 1) for n in (1, 2, 3))
    return (
        jnp.where(lane < 96, parts[0], one),
        jnp.where(lane < 64, one, two),
        jnp.where(lane < 32, two, three),
    )


def turn8(parts):
    slot = lax.broadcasted_iota(jnp.int32, parts[0].shape, 1) // 16
    for step in (1, 2, 4):
        low = (slot // step) % 2 == 0
        turned = list(parts)
        for i in range(8):
            if not i & step:
                first, second = parts[i], parts[i | step]
                turned[i] = jnp.where(low, first, pltpu.roll(second, 16 * step, 1))
                turned[i | step] = jnp.where(low, pltpu.roll(first, 128 - 16 * step, 1), second)
        parts = turned
    return parts


def over_slots(x):
    for step in (16, 32, 64):
        x = x + pltpu.roll(x, step, 1)
    return x


def triangle_kernel(
    nz,
    pair,
    mask,
    norm_gain,
    w_in,
    b_in,
    w_gate,
    b_gate,
    out_gain,
    w_out,
    b_out,
    update,
    nrm,
    wt,
    bias,
    gate,
    flip,
    flop,
    ab,
    recv1,
    zs,
    za,
    zb,
    prods,
    back,
    un,
    land,
    s1,
    r1,
    s2,
    r2a,
    r2b,
    sf,
    rf,
    so,
    ro,
    s3,
    r3,
    s4,
    r4,
):
    nq = 2 * nz
    ci = CHUNK
    channels = nq * nz
    ti, tj, cz = pair.shape
    nch = ti // ci
    row, col = lax.axis_index("row"), lax.axis_index("col")
    z, yl = row // 2, row % 2
    w, core = col // 2, col % 2
    mine = yl * nz + w

    ahead = (nz - SITES) // 2
    site_of = [min(max(place - ahead, 0), SITES - 1) for place in range(nz)]
    group = [(site_of.index(e), site_of.index(e) + site_of.count(e)) for e in range(SITES)]
    shift = [site_of[place] - place + ahead for place in range(nz)]
    n_remote = sum(1 for d in shift if d)

    def along(d):
        return (2 * lax.rem(z + (d + nz) % nz, nz) + yl, col)

    barrier = pltpu.get_barrier_semaphore()

    def greet_plane(t, _):
        dev = lax.rem(yl * nq + col + t, 2 * nq)
        pl.semaphore_signal(
            barrier, inc=1, device_id=(2 * z + dev // nq, dev % nq), device_id_type=MESH
        )
        return 0

    lax.fori_loop(1, 2 * nq, greet_plane, 0)
    for d in range(1, ahead + 1):
        for sign in (1, -1):
            pl.semaphore_signal(barrier, inc=1, device_id=along(sign * d), device_id_type=MESH)

    turned = w_in[...].astype(F32).T.astype(BF16)
    column = jnp.broadcast_to(b_in[...], (LANES, 4 * channels)).T
    for arr in range(2):
        wt[arr] = turned[2 * arr * channels : 2 * (arr + 1) * channels]
        bias[arr] = column[2 * arr * channels : 2 * (arr + 1) * channels]
    nrm[:, tj:, :] = jnp.zeros((ti, LANES - tj, cz), BF16)
    normed = set()

    def front(arr, m):
        fresh = m not in normed
        normed.add(m)

        def step(q, _):
            i0 = m * ci + 4 * q
            if fresh:
                x = pair[pl.ds(i0, 4)].astype(F32)
                centred = x - jnp.mean(x, axis=-1, keepdims=True)
                var = jnp.mean(centred * centred, axis=-1, keepdims=True)
                y = centred * lax.rsqrt(var + 1e-05) * norm_gain[...].reshape(1, 1, cz)
                nrm[pl.ds(i0, 4), 0:tj, :] = y.astype(BF16)
            rhs = nrm[pl.ds(i0, 4)].reshape(4 * LANES, cz)
            res = lax.dot_general(
                wt[arr], rhs, (((1,), (1,)), ((), ())), preferred_element_type=F32
            )
            for t in range(4):
                value = res[0:channels, t * LANES : (t + 1) * LANES] + bias[arr, 0:channels]
                gating = res[channels:, t * LANES : (t + 1) * LANES] + bias[arr, channels:]
                flip[pl.ds(4 * q + t, channels, stride=ci), :] = (
                    mask[pl.ds(i0 + t, 1), :] * sigmoid(gating) * value
                )
            return 0

        lax.fori_loop(0, ci // 4, step, 0, unroll=2)

        def pack(p, _):
            for ch in range(nz):
                ab[arr, m, p, ch] = flip[
                    pl.ds(pl.multiple_of((p * nz + ch) * ci, ci), ci), :
                ].astype(BF16)
            return 0

        lax.fori_loop(0, nq, pack, 0, unroll=2)

    def gates(q, _):
        rows = nrm[pl.ds(4 * q, 4)].reshape(4 * LANES, cz)
        res = jnp.dot(rows, w_gate[...], preferred_element_type=F32) + b_gate[...]
        gate[pl.ds(4 * q, 4)] = sigmoid(res).reshape(4, LANES, cz)[:, 0:tj]
        return 0

    def wait_all(ref, sem):
        pltpu.make_async_copy(ref, ref, sem).wait()

    def send(src, dst, send_sem, recv_sem, device):
        pltpu.make_async_remote_copy(
            src_ref=src,
            dst_ref=dst,
            send_sem=send_sem,
            recv_sem=recv_sem,
            device_id=device,
            device_id_type=MESH,
        ).start()

    def send1(arr, m):
        def step(t, _):
            p = lax.rem(mine + t, nq)
            here = jnp.logical_and(p == mine, core == yl)

            @pl.when(here)
            def _():
                pltpu.make_async_copy(ab.at[arr, m, p], recv1.at[arr, m, col], r1.at[arr, m]).start()

            @pl.when(jnp.logical_not(here))
            def _():
                send(
                    ab.at[arr, m, p],
                    recv1.at[arr, m, col],
                    s1,
                    r1.at[arr, m],
                    (2 * z + p // nz, 2 * (p % nz) + yl),
                )

            return 0

        lax.fori_loop(0, nq, step, 0)

    def enter(arr, m):
        wait_all(recv1.at[arr, m], r1.at[arr, m])

        def step(place, _):
            ch = lax.rem(z - place + ahead + nz, nz)
            for g in range(nq // 4):
                blocks = join4([recv1[arr, m, 4 * g + n, ch].astype(F32) for n in range(4)])
                for n in range(3):
                    zs[arr, m, place, :, (3 * g + n) * LANES : (3 * g + n + 1) * LANES] = blocks[
                        n
                    ].astype(BF16)
            return 0

        lax.fori_loop(0, nz, step, 0)
        for place in sorted(range(nz), key=lambda n: -abs(shift[n])):
            if arr == 0:
                dst = za.at[place, core, m * ci : (m + 1) * ci]
                sem = r2a.at[m]
            else:
                dst = zb.at[site_of[place], m, place]
                sem = r2b.at[m, site_of[place]]
            if shift[place]:
                send(zs.at[arr, m, place], dst, s2, sem, along(shift[place]))
            else:
                pltpu.make_async_copy(zs.at[arr, m, place], dst, sem).start()

    def held(site, m, e):
        return zb.at[site, m, group[e][0] : group[e][1]]

    passed = []

    def pass_on(m, s):
        for site in range(SITES):
            if s == 1:
                wait_all(held(site, m, site), r2b.at[m, site])
            for way, e, to in ((0, site - s + 1, site + 1), (1, site + s - 1, site - 1)):
                if 0 <= e < SITES and 0 <= to < SITES:
                    if s > 1:
                        wait_all(held(site, m, e), rf.at[m, s - 1, site, way])
                    send(
                        held(site, m, e),
                        held(to, m, e),
                        sf,
                        rf.at[m, s, to, way],
                        along(to - site),
                    )
                    passed.append((site, m, e))

    def swap(m):
        part = za.at[:, core, m * ci : (m + 1) * ci]
        return pltpu.make_async_remote_copy(
            src_ref=part,
            dst_ref=part,
            send_sem=so.at[m],
            recv_sem=ro.at[m],
            device_id=(row, 2 * w + 1 - core),
            device_id_type=MESH,
        )

    def product(m):
        for s in range(1, SITES):
            wait_all(held(SITES - 1, m, SITES - 1 - s), rf.at[m, s, SITES - 1, 0])
            wait_all(held(0, m, s), rf.at[m, s, 0, 1])
        for site in range(SITES):
            first, last = group[site]

            rows = (last - first) * 2 * ti
            res = lax.dot_general(
                za[first:last].reshape(rows, za.shape[-1]),
                zb[site, m].reshape(nz * ci, zb.shape[-1]),
                (((1,), (1,)), ((), ())),
                preferred_element_type=F32,
            )
            prods[m, first:last] = res.reshape(last - first, 2, ti, nz * ci).astype(BF16)
        for place in sorted(range(nz), key=lambda n: -abs(shift[n])):
            dst = back.at[m, lax.rem(z - site_of[place] + nz, nz)]
            if shift[place]:
                send(prods.at[m, place], dst, s3, r3.at[m], along(-shift[place]))
            else:
                pltpu.make_async_copy(prods.at[m, place], dst, r3.at[m]).start()

    def turn_and_send(m):
        wait_all(back.at[m], r3.at[m])

        def step(n, _):
            h, rows = n // 3, pl.ds(pl.multiple_of(n % 3 * 32, 32), 32)
            blocks = [
                pltpu.roll(back[m, ch, h, rows].astype(F32), 16 * ((ch - ahead) % 8), 1)
                if ch != ahead
                else back[m, ch, h, rows].astype(F32)
                for ch in range(nz)
            ]
            for n, block in enumerate(turn8(blocks)):
                un[m, h * nz + n, rows] = block.astype(BF16)
            return 0

        lax.fori_loop(0, 6, step, 0)

        def go(t, _):
            p = lax.rem(mine + 1 + t, nq)

            @pl.when(p == mine)
            def _():
                pltpu.make_async_copy(un.at[m, p], land.at[m, mine], r4.at[m]).start()

            @pl.when(p != mine)
            def _():
                send(
                    un.at[m, p],
                    land.at[m, mine],
                    s4,
                    r4.at[m],
                    (2 * z + p // nz, 2 * (p % nz) + core),
                )

            return 0

        lax.fori_loop(0, nq, go, 0)

    def finish(m):
        wait_all(land.at[m], r4.at[m])
        total = jnp.zeros((ti, LANES), F32)
        for p in range(nq):
            total = total + land[m, p].astype(F32)
        mean = over_slots(total) * (1.0 / channels)
        total = jnp.zeros((ti, LANES), F32)
        for p in range(nq):
            centred = land[m, p].astype(F32) - mean
            total = total + centred * centred
        scale = lax.rsqrt(over_slots(total) * (1.0 / channels) + 1e-05)

        def scaled(p, _):
            y = (land[m, p].astype(F32) - mean) * scale * out_gain[pl.ds(p, 1), :]
            y = jnp.concatenate([y, jnp.zeros((LANES - ti, LANES), F32)], axis=0)
            flip[pl.ds(pl.multiple_of(p * LANES, LANES), LANES), :] = y.T
            return 0

        lax.fori_loop(0, nq, scaled, 0, unroll=4)

        def mix(j, _):
            normal = flip[pl.ds(j, channels, stride=ci), :].astype(BF16)
            linear = lax.dot_general(
                normal, w_out[...], (((0,), (0,)), ((), ())), preferred_element_type=F32
            )
            flop[pl.ds(j, ti, stride=ci), :] = linear[0:ti]
            return 0

        lax.fori_loop(0, ci, mix, 0, unroll=4)

        def emit(n, _):
            rows, columns = pl.ds(8 * n, 8), slice(m * ci, (m + 1) * ci)
            linear = flop[pl.ds(pl.multiple_of(8 * n * ci, 8 * ci), 8 * ci), :] + b_out[...]
            update[rows, columns, :] = (
                linear.reshape(8, ci, cz) * gate[rows, columns, :]
            ).astype(BF16)
            return 0

        lax.fori_loop(0, ti // 8, emit, 0, unroll=2)

    order, b_next, a_next = [], 0, 0
    while b_next < nch:
        order.append((1, b_next))
        b_next += 1
        for _ in range(2):
            if a_next < nch:
                order.append((0, a_next))
                a_next += 1

    front(*order[0])
    pl.semaphore_wait(barrier, 2 * nq - 1 + 2 * ahead)
    send1(*order[0])
    front(*order[1])
    send1(*order[1])

    done = {"product": 0, "turn": 0, "finish": 0}
    first_product = 1 + next(m for arr, m in order[order.index((0, nch - 1)) :: -1] if arr)

    def later(k):
        for s in range(1, SITES):
            if 0 <= k - s < nch:
                pass_on(k - s, s)
        if k < first_product:
            return
        if k == first_product:
            for m in range(nch):
                swap(m).wait_recv()
        for n, (name, act) in enumerate(
            (("product", product), ("turn", turn_and_send), ("finish", finish))
        ):
            last = min(k - SITES - n, nch - 1) if k >= first_product + n else -1
            while done[name] <= last:
                act(done[name])
                done[name] += 1

    for n, (arr, m) in enumerate(order):
        enter(arr, m)
        if n + 2 < len(order):
            front(*order[n + 2])
            send1(*order[n + 2])
        if arr == 1:
            later(m)
        elif m:
            wait_all(za.at[:, core, (m - 1) * ci : m * ci], r2a.at[m - 1])
            swap(m - 1).start()
        if (arr, m) == (0, nch - 1):
            lax.fori_loop(0, ti // 4, gates, 0, unroll=2)
            wait_all(za.at[:, core, m * ci :], r2a.at[m])
            swap(m).start()
    for k in range(nch, nch + SITES + 2):
        later(k)

    for arr in range(2):
        for m in range(nch):

            @pl.when(core == yl)
            def _():
                wait_all(ab.at[arr, m, 0 : nq - 1], s1)

            @pl.when(core != yl)
            def _():
                wait_all(ab.at[arr, m], s1)

            wait_all(zs.at[arr, m, 0:n_remote], s2)
    for site, m, e in passed:
        wait_all(held(site, m, e), sf)
    for m in range(nch):
        swap(m).wait_send()
        wait_all(prods.at[m, 0:n_remote], s3)
        wait_all(un.at[m, 0 : nq - 1], s4)


def local(pair, residue_mask, norm_gain, w_in, b_in, w_gate, b_gate, out_gain, w_out, b_out):
    ti, tj, cz = pair.shape
    channels = w_in.shape[1] // 4
    nz = lax.axis_size("row") // 2
    nq = 2 * nz
    ci = CHUNK
    nch = ti // ci
    depth = nq * ti
    valid = residue_mask.astype(F32)
    row_mask = lax.dynamic_slice_in_dim(valid, lax.axis_index("row") * ti, ti)
    col_mask = lax.dynamic_slice_in_dim(valid, lax.axis_index("col") * tj, tj)
    mask = row_mask[:, None] * jnp.pad(col_mask, (0, LANES - tj))[None, :]
    sem = pltpu.SemaphoreType.DMA
    vmem = pl.BlockSpec(memory_space=pltpu.VMEM)
    return pl.pallas_call(
        functools.partial(triangle_kernel, nz),
        out_shape=jax.ShapeDtypeStruct((ti, tj, cz), BF16),
        in_specs=[vmem] * 10,
        out_specs=vmem,
        scratch_shapes=[
            pltpu.VMEM((ti, LANES, cz), BF16),
            pltpu.VMEM((2, 2 * channels, cz), BF16),
            pltpu.VMEM((2, 2 * channels, LANES), F32),
            pltpu.VMEM((ti, tj, cz), F32),
            pltpu.VMEM((channels * ci, LANES), F32),
            pltpu.VMEM((ti * ci, cz), F32),
            pltpu.VMEM((2, nch, nq, nz, ci, LANES), BF16),
            pltpu.VMEM((2, nch, nq, nz, ci, LANES), BF16),
            pltpu.VMEM((2, nch, nz, ci, depth), BF16),
            pltpu.VMEM((nz, 2, ti, depth), BF16),
            pltpu.VMEM((SITES, nch, nz, ci, depth), BF16),
            pltpu.VMEM((nch, nz, 2, ti, nz * ci), BF16),
            pltpu.VMEM((nch, nz, 2, ti, nz * ci), BF16),
            pltpu.VMEM((nch, nq, ti, LANES), BF16),
            pltpu.VMEM((nch, nq, ti, LANES), BF16),
            sem,
            sem((2, nch)),
            sem,
            sem((nch,)),
            sem((nch, SITES)),
            sem,
            sem((nch, SITES, SITES, 2)),
            sem((nch,)),
            sem((nch,)),
            sem,
            sem((nch,)),
            sem,
            sem((nch,)),
        ],
        compiler_params=pltpu.CompilerParams(
            collective_id=0, has_side_effects=True, vmem_limit_bytes=60 * 2**20
        ),
    )(
        pair,
        mask,
        norm_gain.reshape(1, cz),
        w_in,
        b_in.reshape(1, 4 * channels),
        w_gate,
        b_gate.reshape(1, cz),
        jnp.repeat(out_gain, ci).reshape(nq, LANES),
        w_out,
        b_out.reshape(1, cz),
    )


def solution(mesh):
    in_specs = (P("row", "col", None), P(), P(), P(), P(), P(), P(), P(), P(), P())
    out_specs = P("row", "col", None)
    return jax.shard_map(local, mesh=mesh, in_specs=in_specs, out_specs=out_specs, check_vma=False)
```

```python
import functools

import jax
import jax.numpy as jnp
from jax import lax
from jax.experimental import pallas as pl
from jax.experimental.pallas import tpu as pltpu
from jax.sharding import PartitionSpec as P

MESH = pl.DeviceIdType.MESH
BF16 = jnp.bfloat16
F32 = jnp.float32
LANES = 128
CHUNK = 16
SITES = 2


def sigmoid(x):
    return 0.5 * jnp.tanh(0.5 * x) + 0.5


def join4(parts):
    lane = lax.broadcasted_iota(jnp.int32, parts[0].shape, 1)
    one, two, three = (pltpu.roll(parts[n], 128 - 32 * n, 1) for n in (1, 2, 3))
    return (
        jnp.where(lane < 96, parts[0], one),
        jnp.where(lane < 64, one, two),
        jnp.where(lane < 32, two, three),
    )


def turn8(parts):
    slot = lax.broadcasted_iota(jnp.int32, parts[0].shape, 1) // 16
    for step in (1, 2, 4):
        low = (slot // step) % 2 == 0
        turned = list(parts)
        for i in range(8):
            if not i & step:
                first, second = parts[i], parts[i | step]
                turned[i] = jnp.where(low, first, pltpu.roll(second, 16 * step, 1))
                turned[i | step] = jnp.where(low, pltpu.roll(first, 128 - 16 * step, 1), second)
        parts = turned
    return parts


def over_slots(x):
    for step in (16, 32, 64):
        x = x + pltpu.roll(x, step, 1)
    return x


def triangle_kernel(
    nz,
    pair,
    valid,
    norm_gain,
    w_in,
    b_in,
    w_gate,
    b_gate,
    gain,
    w_out,
    b_out,
    update,
    nrm,
    wt,
    bias,
    gate,
    flip,
    flop,
    out_gain,
    ab,
    zf,
    recv1,
    zs,
    za,
    zb,
    prods,
    back,
    un,
    land,
    s1,
    r1,
    sz,
    rz,
    s2,
    r2a,
    r2b,
    sf,
    rf,
    so,
    ro,
    s3,
    r3,
    s4,
    r4,
):
    nq = 2 * nz
    ci = CHUNK
    channels = nq * nz
    ti, tj, cz = pair.shape
    nch = ti // ci
    row, col = lax.axis_index("row"), lax.axis_index("col")
    z, yl = row // 2, row % 2
    w, core = col // 2, col % 2
    mine = yl * nz + w

    ahead = (nz - SITES) // 2
    site_of = [min(max(place - ahead, 0), SITES - 1) for place in range(nz)]
    group = [(site_of.index(e), site_of.index(e) + site_of.count(e)) for e in range(SITES)]
    shift = [site_of[place] - place + ahead for place in range(nz)]
    n_remote = sum(1 for d in shift if d)

    def along(d):
        return (2 * lax.rem(z + (d + nz) % nz, nz) + yl, col)

    barrier = pltpu.get_barrier_semaphore()

    def greet_plane(t, _):
        dev = lax.rem(yl * nq + col + t, 2 * nq)
        pl.semaphore_signal(
            barrier, inc=1, device_id=(2 * z + dev // nq, dev % nq), device_id_type=MESH
        )
        return 0

    lax.fori_loop(1, 2 * nq, greet_plane, 0)
    for d in range(1, ahead + 1):
        for sign in (1, -1):
            pl.semaphore_signal(barrier, inc=1, device_id=along(sign * d), device_id_type=MESH)

    turned = w_in[...].astype(F32).T.astype(BF16)
    column = jnp.broadcast_to(b_in[...], (LANES, 4 * channels)).T
    for arr in range(2):
        wt[arr] = turned[2 * arr * channels : 2 * (arr + 1) * channels]
        bias[arr] = column[2 * arr * channels : 2 * (arr + 1) * channels]
    nrm[:, tj:, :] = jnp.zeros((ti, LANES - tj, cz), BF16)
    lane = lax.broadcasted_iota(jnp.int32, (1, LANES), 1)

    def col_valid(j, mask):
        return jnp.where(lane == j, valid[col * tj + j].astype(F32), mask)

    mask = lax.fori_loop(0, tj, col_valid, jnp.zeros((1, LANES), F32), unroll=8)

    def spread(p, _):
        line = jnp.zeros((1, LANES), F32)
        for ch in range(nz):
            line = jnp.where(lane // ci == ch, gain[p * nz + ch], line)
        out_gain[pl.ds(p, 1), :] = line
        return 0

    lax.fori_loop(0, nq, spread, 0)
    normed = set()

    def front(arr, m):
        fresh = m not in normed
        normed.add(m)

        def step(q, _):
            i0 = m * ci + 4 * q
            if fresh:
                x = pair[pl.ds(i0, 4)].astype(F32)
                centred = x - jnp.mean(x, axis=-1, keepdims=True)
                var = jnp.mean(centred * centred, axis=-1, keepdims=True)
                y = centred * lax.rsqrt(var + 1e-05) * norm_gain[...].reshape(1, 1, cz)
                nrm[pl.ds(i0, 4), 0:tj, :] = y.astype(BF16)
            rhs = nrm[pl.ds(i0, 4)].reshape(4 * LANES, cz)
            res = lax.dot_general(
                wt[arr], rhs, (((1,), (1,)), ((), ())), preferred_element_type=F32
            )
            for t in range(4):
                value = res[0:channels, t * LANES : (t + 1) * LANES] + bias[arr, 0:channels]
                gating = res[channels:, t * LANES : (t + 1) * LANES] + bias[arr, channels:]
                pair_mask = mask * valid[row * ti + i0 + t].astype(F32)
                flip[pl.ds(4 * q + t, channels, stride=ci), :] = (
                    pair_mask * sigmoid(gating) * value
                )
            return 0

        lax.fori_loop(0, ci // 4, step, 0, unroll=2)

        def pack(p, _):
            for ch in range(nz):
                ab[arr, m, p, ch] = flip[
                    pl.ds(pl.multiple_of((p * nz + ch) * ci, ci), ci), :
                ].astype(BF16)
            return 0

        lax.fori_loop(0, nq, pack, 0, unroll=2)

    def gates(q, _):
        rows = nrm[pl.ds(4 * q, 4)].reshape(4 * LANES, cz)
        res = jnp.dot(rows, w_gate[...], preferred_element_type=F32) + b_gate[...]
        gate[pl.ds(4 * q, 4)] = sigmoid(res).reshape(4, LANES, cz)[:, 0:tj]
        return 0

    def wait_all(ref, sem):
        pltpu.make_async_copy(ref, ref, sem).wait()

    def send(src, dst, send_sem, recv_sem, device):
        pltpu.make_async_remote_copy(
            src_ref=src,
            dst_ref=dst,
            send_sem=send_sem,
            recv_sem=recv_sem,
            device_id=device,
            device_id_type=MESH,
        ).start()

    def send1(arr, m, src=None):
        src = ab.at[arr, m] if src is None else src

        def step(t, _):
            p = lax.rem(mine + t, nq)
            here = jnp.logical_and(p == mine, core == yl)

            @pl.when(here)
            def _():
                pltpu.make_async_copy(src.at[p], recv1.at[arr, m, col], r1.at[arr, m]).start()

            @pl.when(jnp.logical_not(here))
            def _():
                send(
                    src.at[p],
                    recv1.at[arr, m, col],
                    s1,
                    r1.at[arr, m],
                    (2 * z + p // nz, 2 * (p % nz) + yl),
                )

            return 0

        lax.fori_loop(0, nq, step, 0)

    far_first = sorted(range(nz), key=lambda place: -abs(shift[place]))

    def z_first():
        for place in far_first:
            src = ab.at[0, 0, :, lax.rem(z - place + ahead + nz, nz)]
            if shift[place]:
                send(src, zf.at[:, place], sz, rz, along(shift[place]))
            else:
                pltpu.make_async_copy(src, zf.at[:, place], rz).start()

    def then_plane():
        wait_all(zf, rz)
        send1(0, 0, zf)

    def enter(arr, m):
        wait_all(recv1.at[arr, m], r1.at[arr, m])

        at_site = (arr, m) == (0, 0)

        def step(place, _):
            block = place if at_site else lax.rem(z - place + ahead + nz, nz)
            for g in range(nq // 4):
                joined = join4([recv1[arr, m, 4 * g + n, block].astype(F32) for n in range(4)])
                for n in range(3):
                    lanes = slice((3 * g + n) * LANES, (3 * g + n + 1) * LANES)
                    if at_site:
                        za[place, core, 0:ci, lanes] = joined[n].astype(BF16)
                    else:
                        zs[arr, m, place, :, lanes] = joined[n].astype(BF16)
            return 0

        lax.fori_loop(0, nz, step, 0)
        if at_site:
            return
        for place in far_first:
            if arr == 0:
                dst = za.at[place, core, m * ci : (m + 1) * ci]
                sem = r2a.at[m]
            else:
                dst = zb.at[site_of[place], m, place]
                sem = r2b.at[m, site_of[place]]
            if shift[place]:
                send(zs.at[arr, m, place], dst, s2, sem, along(shift[place]))
            else:
                pltpu.make_async_copy(zs.at[arr, m, place], dst, sem).start()

    def held(site, m, e):
        return zb.at[site, m, group[e][0] : group[e][1]]

    passed = []

    def pass_on(m, s):
        for site in range(SITES):
            if s == 1:
                wait_all(held(site, m, site), r2b.at[m, site])
            for way, e, to in ((0, site - s + 1, site + 1), (1, site + s - 1, site - 1)):
                if 0 <= e < SITES and 0 <= to < SITES:
                    if s > 1:
                        wait_all(held(site, m, e), rf.at[m, s - 1, site, way])
                    send(
                        held(site, m, e),
                        held(to, m, e),
                        sf,
                        rf.at[m, s, to, way],
                        along(to - site),
                    )
                    passed.append((site, m, e))

    def swap(m):
        part = za.at[:, core, m * ci : (m + 1) * ci]
        return pltpu.make_async_remote_copy(
            src_ref=part,
            dst_ref=part,
            send_sem=so.at[m],
            recv_sem=ro.at[m],
            device_id=(row, 2 * w + 1 - core),
            device_id_type=MESH,
        )

    def product(m):
        for s in range(1, SITES):
            wait_all(held(SITES - 1, m, SITES - 1 - s), rf.at[m, s, SITES - 1, 0])
            wait_all(held(0, m, s), rf.at[m, s, 0, 1])
        for site in range(SITES):
            first, last = group[site]

            rows = (last - first) * 2 * ti
            res = lax.dot_general(
                za[first:last].reshape(rows, za.shape[-1]),
                zb[site, m].reshape(nz * ci, zb.shape[-1]),
                (((1,), (1,)), ((), ())),
                preferred_element_type=F32,
            )
            prods[m, first:last] = res.reshape(last - first, 2, ti, nz * ci).astype(BF16)
        for place in far_first:
            dst = back.at[m, lax.rem(z - site_of[place] + nz, nz)]
            if shift[place]:
                send(prods.at[m, place], dst, s3, r3.at[m], along(-shift[place]))
            else:
                pltpu.make_async_copy(prods.at[m, place], dst, r3.at[m]).start()

    def turn_and_send(m):
        wait_all(back.at[m], r3.at[m])

        def step(n, _):
            h, rows = n // 3, pl.ds(pl.multiple_of(n % 3 * 32, 32), 32)
            blocks = [
                pltpu.roll(back[m, ch, h, rows].astype(F32), 16 * ((ch - ahead) % 8), 1)
                if ch != ahead
                else back[m, ch, h, rows].astype(F32)
                for ch in range(nz)
            ]
            for n, block in enumerate(turn8(blocks)):
                un[m, h * nz + n, rows] = block.astype(BF16)
            return 0

        lax.fori_loop(0, 6, step, 0)

        def go(t, _):
            p = lax.rem(mine + 1 + t, nq)

            @pl.when(p == mine)
            def _():
                pltpu.make_async_copy(un.at[m, p], land.at[m, mine], r4.at[m]).start()

            @pl.when(p != mine)
            def _():
                send(
                    un.at[m, p],
                    land.at[m, mine],
                    s4,
                    r4.at[m],
                    (2 * z + p // nz, 2 * (p % nz) + core),
                )

            return 0

        lax.fori_loop(0, nq, go, 0)

    def finish(m):
        wait_all(land.at[m], r4.at[m])
        total = jnp.zeros((ti, LANES), F32)
        for p in range(nq):
            total = total + land[m, p].astype(F32)
        mean = over_slots(total) * (1.0 / channels)
        total = jnp.zeros((ti, LANES), F32)
        for p in range(nq):
            centred = land[m, p].astype(F32) - mean
            total = total + centred * centred
        scale = lax.rsqrt(over_slots(total) * (1.0 / channels) + 1e-05)

        def scaled(p, _):
            y = (land[m, p].astype(F32) - mean) * scale * out_gain[pl.ds(p, 1), :]
            y = jnp.concatenate([y, jnp.zeros((LANES - ti, LANES), F32)], axis=0)
            flip[pl.ds(pl.multiple_of(p * LANES, LANES), LANES), :] = y.T
            return 0

        lax.fori_loop(0, nq, scaled, 0, unroll=4)

        def mix(j, _):
            normal = flip[pl.ds(j, channels, stride=ci), :].astype(BF16)
            linear = lax.dot_general(
                normal, w_out[...], (((0,), (0,)), ((), ())), preferred_element_type=F32
            )
            flop[pl.ds(j, ti, stride=ci), :] = linear[0:ti]
            return 0

        lax.fori_loop(0, ci, mix, 0, unroll=4)

        def emit(n, _):
            rows, columns = pl.ds(8 * n, 8), slice(m * ci, (m + 1) * ci)
            linear = flop[pl.ds(pl.multiple_of(8 * n * ci, 8 * ci), 8 * ci), :] + b_out[...]
            update[rows, columns, :] = (
                linear.reshape(8, ci, cz) * gate[rows, columns, :]
            ).astype(BF16)
            return 0

        lax.fori_loop(0, ti // 8, emit, 0, unroll=2)

    def join_swap(m):
        if m:
            wait_all(za.at[:, core, m * ci : (m + 1) * ci], r2a.at[m])
        swap(m).start()

    def all_gates():
        lax.fori_loop(0, ti // 4, gates, 0, unroll=2)

    def all_of_a():
        for m in range(nch):
            swap(m).wait_recv()

    first = [(0, 0), (1, 0), (0, 1), (1, 1)]
    for chunk in first:
        front(*chunk)
    pl.semaphore_wait(barrier, 2 * nq - 1 + 2 * ahead)
    plan = [
        (z_first,),
        (send1, 1, 0),
        (send1, 0, 1),
        (front, 0, 2),
        (enter, 1, 0),
        (send1, 1, 1),
        (front, 0, 3),
        (front, 1, 2),
        (then_plane,),
        (enter, 0, 1),
        (send1, 0, 2),
        (front, 0, 4),
        (pass_on, 0, 1),
        (enter, 1, 1),
        (send1, 0, 3),
        (front, 0, 5),
        (enter, 0, 2),
        (send1, 1, 2),
        (enter, 0, 0),
        (join_swap, 0),
        (join_swap, 1),
        (front, 1, 3),
        (pass_on, 1, 1),
        (enter, 0, 3),
        (send1, 0, 4),
        (front, 1, 4),
        (join_swap, 2),
        (all_gates,),
        (enter, 1, 2),
        (send1, 0, 5),
        (front, 1, 5),
        (enter, 0, 4),
        (send1, 1, 3),
        (join_swap, 3),
        (enter, 0, 5),
        (send1, 1, 4),
        (pass_on, 2, 1),
        (enter, 1, 3),
        (send1, 1, 5),
        (join_swap, 4),
        (enter, 1, 4),
        (join_swap, 5),
        (enter, 1, 5),
        (all_of_a,),
        (product, 0),
        (product, 1),
        (pass_on, 3, 1),
        (product, 2),
        (pass_on, 4, 1),
        (pass_on, 5, 1),
        (turn_and_send, 0),
        (turn_and_send, 1),
        (finish, 0),
        (turn_and_send, 2),
        (finish, 1),
        (product, 3),
        (finish, 2),
        (product, 4),
        (product, 5),
        (turn_and_send, 3),
        (turn_and_send, 4),
        (finish, 3),
        (turn_and_send, 5),
        (finish, 4),
        (finish, 5),
    ]
    for act, *which in plan:
        act(*which)

    for arr in range(2):
        for m in range(nch):

            @pl.when(core == yl)
            def _():
                wait_all(ab.at[arr, m, 0 : nq - 1], s1)

            @pl.when(core != yl)
            def _():
                wait_all(ab.at[arr, m], s1)

            if (arr, m) != (0, 0):
                wait_all(zs.at[arr, m, 0:n_remote], s2)
    wait_all(zf.at[:, 0:n_remote], sz)
    for site, m, e in passed:
        wait_all(held(site, m, e), sf)
    for m in range(nch):
        swap(m).wait_send()
        wait_all(prods.at[m, 0:n_remote], s3)
        wait_all(un.at[m, 0 : nq - 1], s4)


def local(pair, residue_mask, norm_gain, w_in, b_in, w_gate, b_gate, out_gain, w_out, b_out):
    ti, tj, cz = pair.shape
    channels = w_in.shape[1] // 4
    nz = lax.axis_size("row") // 2
    nq = 2 * nz
    ci = CHUNK
    nch = ti // ci
    depth = nq * ti
    sem = pltpu.SemaphoreType.DMA
    vmem = pl.BlockSpec(memory_space=pltpu.VMEM)
    smem = pl.BlockSpec(memory_space=pltpu.SMEM)
    return pl.pallas_call(
        functools.partial(triangle_kernel, nz),
        out_shape=jax.ShapeDtypeStruct((ti, tj, cz), BF16),
        in_specs=[vmem, smem] + [vmem] * 5 + [smem] + [vmem] * 2,
        out_specs=vmem,
        scratch_shapes=[
            pltpu.VMEM((ti, LANES, cz), BF16),
            pltpu.VMEM((2, 2 * channels, cz), BF16),
            pltpu.VMEM((2, 2 * channels, LANES), F32),
            pltpu.VMEM((ti, tj, cz), F32),
            pltpu.VMEM((channels * ci, LANES), F32),
            pltpu.VMEM((ti * ci, cz), F32),
            pltpu.VMEM((nq, LANES), F32),
            pltpu.VMEM((2, nch, nq, nz, ci, LANES), BF16),
            pltpu.VMEM((nq, nz, ci, LANES), BF16),
            pltpu.VMEM((2, nch, nq, nz, ci, LANES), BF16),
            pltpu.VMEM((2, nch, nz, ci, depth), BF16),
            pltpu.VMEM((nz, 2, ti, depth), BF16),
            pltpu.VMEM((SITES, nch, nz, ci, depth), BF16),
            pltpu.VMEM((nch, nz, 2, ti, nz * ci), BF16),
            pltpu.VMEM((nch, nz, 2, ti, nz * ci), BF16),
            pltpu.VMEM((nch, nq, ti, LANES), BF16),
            pltpu.VMEM((nch, nq, ti, LANES), BF16),
            sem,
            sem((2, nch)),
            sem,
            sem,
            sem,
            sem((nch,)),
            sem((nch, SITES)),
            sem,
            sem((nch, SITES, SITES, 2)),
            sem((nch,)),
            sem((nch,)),
            sem,
            sem((nch,)),
            sem,
            sem((nch,)),
        ],
        compiler_params=pltpu.CompilerParams(
            collective_id=0, has_side_effects=True, vmem_limit_bytes=60 * 2**20
        ),
    )(
        pair,
        residue_mask,
        norm_gain.reshape(1, cz),
        w_in,
        b_in.reshape(1, 4 * channels),
        w_gate,
        b_gate.reshape(1, cz),
        out_gain,
        w_out,
        b_out.reshape(1, cz),
    )


def solution(mesh):
    in_specs = (P("row", "col", None), P(), P(), P(), P(), P(), P(), P(), P(), P())
    out_specs = P("row", "col", None)
    return jax.shard_map(local, mesh=mesh, in_specs=in_specs, out_specs=out_specs, check_vma=False)
```

```python
import functools

import jax
import jax.numpy as jnp
from jax import lax
from jax.experimental import pallas as pl
from jax.experimental.pallas import tpu as pltpu
from jax.sharding import PartitionSpec as P

MESH = pl.DeviceIdType.MESH
BF16 = jnp.bfloat16
F32 = jnp.float32
LANES = 128
CHUNK = 16
SITES = 2


def sigmoid(x):
    return 0.5 * jnp.tanh(0.5 * x) + 0.5


def join4(parts):
    lane = lax.broadcasted_iota(jnp.int32, parts[0].shape, 1)
    one, two, three = (pltpu.roll(parts[n], 128 - 32 * n, 1) for n in (1, 2, 3))
    return (
        jnp.where(lane < 96, parts[0], one),
        jnp.where(lane < 64, one, two),
        jnp.where(lane < 32, two, three),
    )


def turn8(parts):
    slot = lax.broadcasted_iota(jnp.int32, parts[0].shape, 1) // 16
    for step in (1, 2, 4):
        low = (slot // step) % 2 == 0
        turned = list(parts)
        for i in range(8):
            if not i & step:
                first, second = parts[i], parts[i | step]
                turned[i] = jnp.where(low, first, pltpu.roll(second, 16 * step, 1))
                turned[i | step] = jnp.where(low, pltpu.roll(first, 128 - 16 * step, 1), second)
        parts = turned
    return parts


def over_slots(x):
    for step in (16, 32, 64):
        x = x + pltpu.roll(x, step, 1)
    return x


def triangle_kernel(
    nz,
    pair_in,
    valid,
    norm_gain,
    w_in,
    b_in,
    w_gate,
    b_gate,
    gain,
    w_out,
    b_out,
    update,
    pair,
    sp,
    nrm,
    wt,
    bias,
    gate,
    flip,
    flop,
    out_gain,
    late_gain,
    w_late,
    ab,
    zf,
    recv1,
    zs,
    za,
    zb,
    prods,
    back,
    un,
    land,
    mid,
    rm,
    s1,
    r1,
    sz,
    rz,
    s2,
    r2a,
    r2b,
    sf,
    rf,
    so,
    ro,
    s3,
    r3,
    s4,
    r4,
):
    nq = 2 * nz
    ci = CHUNK
    channels = nq * nz
    ti, tj, cz = pair.shape
    nch = ti // ci
    row, col = lax.axis_index("row"), lax.axis_index("col")
    z, yl = row // 2, row % 2
    w, core = col // 2, col % 2
    mine = yl * nz + w

    ahead = (nz - SITES) // 2
    site_of = [min(max(place - ahead, 0), SITES - 1) for place in range(nz)]
    group = [(site_of.index(e), site_of.index(e) + site_of.count(e)) for e in range(SITES)]
    shift = [site_of[place] - place + ahead for place in range(nz)]
    n_remote = sum(1 for d in shift if d)

    def along(d):
        return (2 * lax.rem(z + (d + nz) % nz, nz) + yl, col)

    barrier = pltpu.get_barrier_semaphore()

    def greet_plane(t, _):
        dev = lax.rem(yl * nq + col + t, 2 * nq)
        pl.semaphore_signal(
            barrier, inc=1, device_id=(2 * z + dev // nq, dev % nq), device_id_type=MESH
        )
        return 0

    lax.fori_loop(1, 2 * nq, greet_plane, 0)
    for d in range(1, ahead + 1):
        for sign in (1, -1):
            pl.semaphore_signal(barrier, inc=1, device_id=along(sign * d), device_id_type=MESH)

    load = pltpu.make_async_copy(pair_in, pair, sp)
    load.start()

    turned = w_in[...].astype(F32).T.astype(BF16)
    column = jnp.broadcast_to(b_in[...], (LANES, 4 * channels)).T
    for arr in range(2):
        wt[arr] = turned[2 * arr * channels : 2 * (arr + 1) * channels]
        bias[arr] = column[2 * arr * channels : 2 * (arr + 1) * channels]
    nrm[:, tj:, :] = jnp.zeros((ti, LANES - tj, cz), BF16)
    lane = lax.broadcasted_iota(jnp.int32, (1, LANES), 1)

    def col_valid(j, mask):
        return jnp.where(lane == j, valid[col * tj + j].astype(F32), mask)

    mask = lax.fori_loop(0, tj, col_valid, jnp.zeros((1, LANES), F32), unroll=8)

    def spread(p, _):
        line = jnp.zeros((1, LANES), F32)
        for ch in range(nz):
            line = jnp.where(lane // ci == ch, gain[p * nz + ch], line)
        out_gain[pl.ds(p, 1), :] = line
        line = jnp.zeros((1, LANES), F32)
        for n in range(nz):
            line = jnp.where(lane // ci == n, gain[(p % 2 * nz + n) * nz + p // 2], line)
        late_gain[pl.ds(p, 1), :] = line
        return 0

    lax.fori_loop(0, nq, spread, 0)
    flop[0:channels, :] = w_out[...].astype(F32)
    for ch in range(nz):
        w_late[ch * nq : (ch + 1) * nq] = flop[pl.ds(ch, nq, stride=nz), :].astype(BF16)
    normed = set()

    def front(arr, m):
        fresh = m not in normed
        normed.add(m)

        def step(q, _):
            i0 = m * ci + 4 * q
            if fresh:
                x = pair[pl.ds(i0, 4)].astype(F32)
                centred = x - jnp.mean(x, axis=-1, keepdims=True)
                var = jnp.mean(centred * centred, axis=-1, keepdims=True)
                y = centred * lax.rsqrt(var + 1e-05) * norm_gain[...].reshape(1, 1, cz)
                nrm[pl.ds(i0, 4), 0:tj, :] = y.astype(BF16)
            rhs = nrm[pl.ds(i0, 4)].reshape(4 * LANES, cz)
            res = lax.dot_general(
                wt[arr], rhs, (((1,), (1,)), ((), ())), preferred_element_type=F32
            )
            for t in range(4):
                value = res[0:channels, t * LANES : (t + 1) * LANES] + bias[arr, 0:channels]
                gating = res[channels:, t * LANES : (t + 1) * LANES] + bias[arr, channels:]
                pair_mask = mask * valid[row * ti + i0 + t].astype(F32)
                flip[pl.ds(4 * q + t, channels, stride=ci), :] = (
                    pair_mask * sigmoid(gating) * value
                )
            return 0

        lax.fori_loop(0, ci // 4, step, 0, unroll=2)

        def pack(p, _):
            for ch in range(nz):
                ab[arr, m, p, ch] = flip[
                    pl.ds(pl.multiple_of((p * nz + ch) * ci, ci), ci), :
                ].astype(BF16)
            return 0

        lax.fori_loop(0, nq, pack, 0, unroll=2)

    def gates(q, _):
        rows = nrm[pl.ds(4 * q, 4)].reshape(4 * LANES, cz)
        res = jnp.dot(rows, w_gate[...], preferred_element_type=F32) + b_gate[...]
        gate[pl.ds(4 * q, 4)] = sigmoid(res).reshape(4, LANES, cz)[:, 0:tj]
        return 0

    def wait_all(ref, sem):
        pltpu.make_async_copy(ref, ref, sem).wait()

    def send(src, dst, send_sem, recv_sem, device):
        pltpu.make_async_remote_copy(
            src_ref=src,
            dst_ref=dst,
            send_sem=send_sem,
            recv_sem=recv_sem,
            device_id=device,
            device_id_type=MESH,
        ).start()

    def send1(arr, m, src=None):
        src = ab.at[arr, m] if src is None else src

        def step(t, _):
            p = lax.rem(mine + t, nq)
            here = jnp.logical_and(p == mine, core == yl)

            @pl.when(here)
            def _():
                pltpu.make_async_copy(src.at[p], recv1.at[arr, m, col], r1.at[arr, m]).start()

            @pl.when(jnp.logical_not(here))
            def _():
                send(
                    src.at[p],
                    recv1.at[arr, m, col],
                    s1,
                    r1.at[arr, m],
                    (2 * z + p // nz, 2 * (p % nz) + yl),
                )

            return 0

        lax.fori_loop(0, nq, step, 0)

    far_first = sorted(range(nz), key=lambda place: -abs(shift[place]))

    def z_first():
        for place in far_first:
            src = ab.at[0, 0, :, lax.rem(z - place + ahead + nz, nz)]
            if shift[place]:
                send(src, zf.at[:, place], sz, rz, along(shift[place]))
            else:
                pltpu.make_async_copy(src, zf.at[:, place], rz).start()

    def then_plane():
        wait_all(zf, rz)
        send1(0, 0, zf)

    def enter(arr, m):
        wait_all(recv1.at[arr, m], r1.at[arr, m])

        at_site = (arr, m) == (0, 0)

        def step(place, _):
            block = place if at_site else lax.rem(z - place + ahead + nz, nz)
            for g in range(nq // 4):
                joined = join4([recv1[arr, m, 4 * g + n, block].astype(F32) for n in range(4)])
                for n in range(3):
                    lanes = slice((3 * g + n) * LANES, (3 * g + n + 1) * LANES)
                    if at_site:
                        za[place, core, 0:ci, lanes] = joined[n].astype(BF16)
                    else:
                        zs[arr, m, place, :, lanes] = joined[n].astype(BF16)
            return 0

        lax.fori_loop(0, nz, step, 0)
        if at_site:
            return
        for place in far_first:
            if arr == 0:
                dst = za.at[place, core, m * ci : (m + 1) * ci]
                sem = r2a.at[m]
            else:
                dst = zb.at[site_of[place], m, place]
                sem = r2b.at[m, site_of[place]]
            if shift[place]:
                send(zs.at[arr, m, place], dst, s2, sem, along(shift[place]))
            else:
                pltpu.make_async_copy(zs.at[arr, m, place], dst, sem).start()

    def held(site, m, e):
        return zb.at[site, m, group[e][0] : group[e][1]]

    passed = []

    def pass_on(m, s):
        for site in range(SITES):
            if s == 1:
                wait_all(held(site, m, site), r2b.at[m, site])
            for way, e, to in ((0, site - s + 1, site + 1), (1, site + s - 1, site - 1)):
                if 0 <= e < SITES and 0 <= to < SITES:
                    if s > 1:
                        wait_all(held(site, m, e), rf.at[m, s - 1, site, way])
                    send(
                        held(site, m, e),
                        held(to, m, e),
                        sf,
                        rf.at[m, s, to, way],
                        along(to - site),
                    )
                    passed.append((site, m, e))

    def swap(m):
        part = za.at[:, core, m * ci : (m + 1) * ci]
        return pltpu.make_async_remote_copy(
            src_ref=part,
            dst_ref=part,
            send_sem=so.at[m],
            recv_sem=ro.at[m],
            device_id=(row, 2 * w + 1 - core),
            device_id_type=MESH,
        )

    def product(m):
        for s in range(1, SITES):
            wait_all(held(SITES - 1, m, SITES - 1 - s), rf.at[m, s, SITES - 1, 0])
            wait_all(held(0, m, s), rf.at[m, s, 0, 1])
        for site in range(SITES):
            first, last = group[site]

            rows = (last - first) * 2 * ti
            res = lax.dot_general(
                za[first:last].reshape(rows, za.shape[-1]),
                zb[site, m].reshape(nz * ci, zb.shape[-1]),
                (((1,), (1,)), ((), ())),
                preferred_element_type=F32,
            )
            prods[m, first:last] = res.reshape(last - first, 2, ti, nz * ci).astype(BF16)
        if m < nch - 1:
            send_back(m)

    def send_back(m):
        for place in far_first:
            dst = back.at[m, lax.rem(z - site_of[place] + nz, nz)]
            if shift[place]:
                send(prods.at[m, place], dst, s3, r3.at[m], along(-shift[place]))
            else:
                pltpu.make_async_copy(prods.at[m, place], dst, r3.at[m]).start()

    def turn(m, load_block, store_block):
        def step(n, _):
            h, rows = n // 3, pl.ds(pl.multiple_of(n % 3 * 32, 32), 32)
            for i, block in enumerate(turn8([load_block(i, h, rows) for i in range(nz)])):
                store_block(i, h, rows, block.astype(BF16))
            return 0

        lax.fori_loop(0, 6, step, 0)

    def to_plane(m, dst, sem):
        def go(t, _):
            p = lax.rem(mine + 1 + t, nq)

            @pl.when(p == mine)
            def _():
                pltpu.make_async_copy(un.at[m, p], dst.at[mine], sem).start()

            @pl.when(p != mine)
            def _():
                device = (2 * z + p // nz, 2 * (p % nz) + core)
                send(un.at[m, p], dst.at[mine], s4, sem, device)

            return 0

        lax.fori_loop(0, nq, go, 0)

    def store_un(m):
        def store(i, h, rows, block):
            un[m, h * nz + i, rows] = block

        return store

    def turn_and_send(m):
        wait_all(back.at[m], r3.at[m])

        def load_block(ch, h, rows):
            block = back[m, ch, h, rows].astype(F32)
            return pltpu.roll(block, 16 * ((ch - ahead) % nz), 1) if ch != ahead else block

        turn(m, load_block, store_un(m))
        to_plane(m, land.at[m], r4.at[m])

    def turn_at_site(m):
        def load_block(place, h, rows):
            amount = 16 * lax.rem(z - site_of[place] - ahead + 2 * nz, nz)
            return pltpu.roll(prods[m, place, h, rows].astype(F32), amount, 1)

        turn(m, load_block, store_un(m))
        to_plane(m, mid, rm)

    def turn_and_return(m):
        wait_all(mid, rm)

        def load_block(n, half, rows):
            return mid[half * nz + n, rows].astype(F32)

        def store_block(place, half, rows, block):
            prods[m, place, half, rows] = block

        turn(m, load_block, store_block)
        send_back(m)

    def finish(m):
        late = m == nch - 1
        if late:
            wait_all(back.at[m], r3.at[m])
        else:
            wait_all(land.at[m], r4.at[m])
        gains, weights = (late_gain, w_late) if late else (out_gain, w_out)

        def block(p):
            return (back[m, p // 2, p % 2] if late else land[m, p]).astype(F32)

        total = jnp.zeros((ti, LANES), F32)
        for p in range(nq):
            total = total + block(p)
        mean = over_slots(total) * (1.0 / channels)
        total = jnp.zeros((ti, LANES), F32)
        for p in range(nq):
            centred = block(p) - mean
            total = total + centred * centred
        scale = lax.rsqrt(over_slots(total) * (1.0 / channels) + 1e-05)

        def scaled(p, _):
            y = (block(p) - mean) * scale * gains[pl.ds(p, 1), :]
            y = jnp.concatenate([y, jnp.zeros((LANES - ti, LANES), F32)], axis=0)
            flip[pl.ds(pl.multiple_of(p * LANES, LANES), LANES), :] = y.T
            return 0

        lax.fori_loop(0, nq, scaled, 0, unroll=4)

        def mix(j, _):
            normal = flip[pl.ds(j, channels, stride=ci), :].astype(BF16)
            linear = lax.dot_general(
                normal, weights[...], (((0,), (0,)), ((), ())), preferred_element_type=F32
            )
            flop[pl.ds(j, ti, stride=ci), :] = linear[0:ti]
            return 0

        lax.fori_loop(0, ci, mix, 0, unroll=4)

        def emit(n, _):
            rows, columns = pl.ds(8 * n, 8), slice(m * ci, (m + 1) * ci)
            linear = flop[pl.ds(pl.multiple_of(8 * n * ci, 8 * ci), 8 * ci), :] + b_out[...]
            update[rows, columns, :] = (
                linear.reshape(8, ci, cz) * gate[rows, columns, :]
            ).astype(BF16)
            return 0

        lax.fori_loop(0, ti // 8, emit, 0, unroll=2)

    def join_swap(m):
        if m:
            wait_all(za.at[:, core, m * ci : (m + 1) * ci], r2a.at[m])
        swap(m).start()

    def all_gates():
        lax.fori_loop(0, ti // 4, gates, 0, unroll=2)

    def all_of_a():
        for m in range(nch):
            swap(m).wait_recv()

    first = [(0, 0), (1, 0)]
    load.wait()
    for chunk in first:
        front(*chunk)
    pl.semaphore_wait(barrier, 2 * nq - 1 + 2 * ahead)
    plan = [
        (z_first,),
        (send1, 1, 0),
        (front, 0, 1),
        (send1, 0, 1),
        (front, 1, 1),
        (front, 0, 2),
        (enter, 1, 0),
        (send1, 1, 1),
        (front, 0, 3),
        (front, 1, 2),
        (then_plane,),
        (enter, 0, 1),
        (send1, 0, 2),
        (front, 0, 4),
        (pass_on, 0, 1),
        (enter, 1, 1),
        (send1, 0, 3),
        (front, 0, 5),
        (enter, 0, 2),
        (send1, 1, 2),
        (enter, 0, 0),
        (join_swap, 0),
        (join_swap, 1),
        (front, 1, 3),
        (pass_on, 1, 1),
        (enter, 0, 3),
        (send1, 0, 4),
        (front, 1, 4),
        (join_swap, 2),
        (all_gates,),
        (enter, 1, 2),
        (send1, 0, 5),
        (front, 1, 5),
        (enter, 0, 4),
        (send1, 1, 3),
        (join_swap, 3),
        (enter, 0, 5),
        (send1, 1, 4),
        (pass_on, 2, 1),
        (enter, 1, 3),
        (send1, 1, 5),
        (join_swap, 4),
        (enter, 1, 4),
        (join_swap, 5),
        (enter, 1, 5),
        (all_of_a,),
        (product, 0),
        (product, 1),
        (pass_on, 3, 1),
        (product, 2),
        (pass_on, 4, 1),
        (pass_on, 5, 1),
        (turn_and_send, 0),
        (turn_and_send, 1),
        (finish, 0),
        (turn_and_send, 2),
        (finish, 1),
        (product, 3),
        (finish, 2),
        (product, 4),
        (product, 5),
        (turn_at_site, 5),
        (turn_and_send, 3),
        (turn_and_return, 5),
        (turn_and_send, 4),
        (finish, 3),
        (finish, 4),
        (finish, 5),
    ]
    for act, *which in plan:
        act(*which)

    for arr in range(2):
        for m in range(nch):

            @pl.when(core == yl)
            def _():
                wait_all(ab.at[arr, m, 0 : nq - 1], s1)

            @pl.when(core != yl)
            def _():
                wait_all(ab.at[arr, m], s1)

            if (arr, m) != (0, 0):
                wait_all(zs.at[arr, m, 0:n_remote], s2)
    wait_all(zf.at[:, 0:n_remote], sz)
    for site, m, e in passed:
        wait_all(held(site, m, e), sf)
    for m in range(nch):
        swap(m).wait_send()
        wait_all(prods.at[m, 0:n_remote], s3)
        wait_all(un.at[m, 0 : nq - 1], s4)


def local(pair, residue_mask, norm_gain, w_in, b_in, w_gate, b_gate, out_gain, w_out, b_out):
    ti, tj, cz = pair.shape
    channels = w_in.shape[1] // 4
    nz = lax.axis_size("row") // 2
    nq = 2 * nz
    ci = CHUNK
    nch = ti // ci
    depth = nq * ti
    sem = pltpu.SemaphoreType.DMA
    vmem = pl.BlockSpec(memory_space=pltpu.VMEM)
    smem = pl.BlockSpec(memory_space=pltpu.SMEM)
    return pl.pallas_call(
        functools.partial(triangle_kernel, nz),
        out_shape=jax.ShapeDtypeStruct((ti, tj, cz), BF16),
        in_specs=[pl.BlockSpec(memory_space=pl.ANY), smem] + [vmem] * 5 + [smem] + [vmem] * 2,
        out_specs=vmem,
        scratch_shapes=[
            pltpu.VMEM((ti, tj, cz), BF16),
            sem,
            pltpu.VMEM((ti, LANES, cz), BF16),
            pltpu.VMEM((2, 2 * channels, cz), BF16),
            pltpu.VMEM((2, 2 * channels, LANES), F32),
            pltpu.VMEM((ti, tj, cz), F32),
            pltpu.VMEM((channels * ci, LANES), F32),
            pltpu.VMEM((ti * ci, cz), F32),
            pltpu.VMEM((nq, LANES), F32),
            pltpu.VMEM((nq, LANES), F32),
            pltpu.VMEM((channels, cz), BF16),
            pltpu.VMEM((2, nch, nq, nz, ci, LANES), BF16),
            pltpu.VMEM((nq, nz, ci, LANES), BF16),
            pltpu.VMEM((2, nch, nq, nz, ci, LANES), BF16),
            pltpu.VMEM((2, nch, nz, ci, depth), BF16),
            pltpu.VMEM((nz, 2, ti, depth), BF16),
            pltpu.VMEM((SITES, nch, nz, ci, depth), BF16),
            pltpu.VMEM((nch, nz, 2, ti, nz * ci), BF16),
            pltpu.VMEM((nch, nz, 2, ti, nz * ci), BF16),
            pltpu.VMEM((nch, nq, ti, LANES), BF16),
            pltpu.VMEM((nch, nq, ti, LANES), BF16),
            pltpu.VMEM((nq, ti, LANES), BF16),
            sem,
            sem,
            sem((2, nch)),
            sem,
            sem,
            sem,
            sem((nch,)),
            sem((nch, SITES)),
            sem,
            sem((nch, SITES, SITES, 2)),
            sem((nch,)),
            sem((nch,)),
            sem,
            sem((nch,)),
            sem,
            sem((nch,)),
        ],
        compiler_params=pltpu.CompilerParams(
            collective_id=0, has_side_effects=True, vmem_limit_bytes=60 * 2**20
        ),
    )(
        pair,
        residue_mask,
        norm_gain.reshape(1, cz),
        w_in,
        b_in.reshape(1, 4 * channels),
        w_gate,
        b_gate.reshape(1, cz),
        out_gain,
        w_out,
        b_out.reshape(1, cz),
    )


def solution(mesh):
    in_specs = (P("row", "col", None), P(), P(), P(), P(), P(), P(), P(), P(), P())
    out_specs = P("row", "col", None)
    return jax.shard_map(local, mesh=mesh, in_specs=in_specs, out_specs=out_specs, check_vma=False)
```

```python
import functools

import jax
import jax.numpy as jnp
from jax import lax
from jax.experimental import pallas as pl
from jax.experimental.pallas import tpu as pltpu
from jax.sharding import PartitionSpec as P

MESH = pl.DeviceIdType.MESH
BF16 = jnp.bfloat16
F32 = jnp.float32
LANES = 128
CHUNK = 16
SITES = 2


def sigmoid(x):
    return 0.5 * jnp.tanh(0.5 * x) + 0.5


def join4(parts):
    lane = lax.broadcasted_iota(jnp.int32, parts[0].shape, 1)
    one, two, three = (pltpu.roll(parts[n], 128 - 32 * n, 1) for n in (1, 2, 3))
    return (
        jnp.where(lane < 96, parts[0], one),
        jnp.where(lane < 64, one, two),
        jnp.where(lane < 32, two, three),
    )


def turn8(parts):
    slot = lax.broadcasted_iota(jnp.int32, parts[0].shape, 1) // 16
    for step in (1, 2, 4):
        low = (slot // step) % 2 == 0
        turned = list(parts)
        for i in range(8):
            if not i & step:
                first, second = parts[i], parts[i | step]
                turned[i] = jnp.where(low, first, pltpu.roll(second, 16 * step, 1))
                turned[i | step] = jnp.where(low, pltpu.roll(first, 128 - 16 * step, 1), second)
        parts = turned
    return parts


def over_slots(x):
    for step in (16, 32, 64):
        x = x + pltpu.roll(x, step, 1)
    return x


def triangle_kernel(
    nz,
    pair_in,
    valid,
    norm_gain,
    w_in,
    b_in,
    w_gate,
    b_gate,
    gain,
    w_out,
    b_out,
    update,
    pair,
    sp,
    nrm,
    wt,
    bias,
    gate,
    flip,
    flop,
    out_gain,
    late_gain,
    w_late,
    ab,
    zf,
    recv1,
    zs,
    za,
    zb,
    prods,
    back,
    un,
    land,
    mid,
    rm,
    s1,
    r1,
    sz,
    rz,
    s2,
    r2a,
    r2b,
    sf,
    rf,
    so,
    ro,
    s3,
    r3,
    s4,
    r4,
):
    nq = 2 * nz
    ci = CHUNK
    channels = nq * nz
    ti, tj, cz = pair.shape
    nch = ti // ci
    row, col = lax.axis_index("row"), lax.axis_index("col")
    z, yl = row // 2, row % 2
    w, core = col // 2, col % 2
    mine = yl * nz + w

    ahead = (nz - SITES) // 2
    site_of = [min(max(place - ahead, 0), SITES - 1) for place in range(nz)]
    group = [(site_of.index(e), site_of.index(e) + site_of.count(e)) for e in range(SITES)]
    shift = [site_of[place] - place + ahead for place in range(nz)]
    n_remote = sum(1 for d in shift if d)

    def along(d):
        return (2 * lax.rem(z + (d + nz) % nz, nz) + yl, col)

    barrier = pltpu.get_barrier_semaphore()

    def greet_plane(t, _):
        dev = lax.rem(yl * nq + col + t, 2 * nq)
        pl.semaphore_signal(
            barrier, inc=1, device_id=(2 * z + dev // nq, dev % nq), device_id_type=MESH
        )
        return 0

    lax.fori_loop(1, 2 * nq, greet_plane, 0)
    for d in range(1, ahead + 1):
        for sign in (1, -1):
            pl.semaphore_signal(barrier, inc=1, device_id=along(sign * d), device_id_type=MESH)

    load = pltpu.make_async_copy(pair_in, pair, sp)
    load.start()

    turned = w_in[...].astype(F32).T.astype(BF16)
    column = jnp.broadcast_to(b_in[...], (LANES, 4 * channels)).T
    for arr in range(2):
        wt[arr] = turned[2 * arr * channels : 2 * (arr + 1) * channels]
        bias[arr] = column[2 * arr * channels : 2 * (arr + 1) * channels]
    nrm[:, tj:, :] = jnp.zeros((ti, LANES - tj, cz), BF16)
    lane = lax.broadcasted_iota(jnp.int32, (1, LANES), 1)

    def col_valid(j, mask):
        return jnp.where(lane == j, valid[col * tj + j].astype(F32), mask)

    mask = lax.fori_loop(0, tj, col_valid, jnp.zeros((1, LANES), F32), unroll=8)

    def spread(p, _):
        line = jnp.zeros((1, LANES), F32)
        for ch in range(nz):
            line = jnp.where(lane // ci == ch, gain[p * nz + ch], line)
        out_gain[pl.ds(p, 1), :] = line
        line = jnp.zeros((1, LANES), F32)
        for n in range(nz):
            line = jnp.where(lane // ci == n, gain[(p % 2 * nz + n) * nz + p // 2], line)
        late_gain[pl.ds(p, 1), :] = line
        return 0

    lax.fori_loop(0, nq, spread, 0)
    flop[0:channels, :] = w_out[...].astype(F32)
    for ch in range(nz):
        w_late[ch * nq : (ch + 1) * nq] = flop[pl.ds(ch, nq, stride=nz), :].astype(BF16)
    normed = set()

    def front(arr, m):
        fresh = m not in normed
        normed.add(m)

        def step(q, _):
            i0 = m * ci + 4 * q
            if fresh:
                x = pair[pl.ds(i0, 4)].astype(F32)
                centred = x - jnp.mean(x, axis=-1, keepdims=True)
                var = jnp.mean(centred * centred, axis=-1, keepdims=True)
                y = centred * lax.rsqrt(var + 1e-05) * norm_gain[...].reshape(1, 1, cz)
                nrm[pl.ds(i0, 4), 0:tj, :] = y.astype(BF16)
            rhs = nrm[pl.ds(i0, 4)].reshape(4 * LANES, cz)
            res = lax.dot_general(
                wt[arr], rhs, (((1,), (1,)), ((), ())), preferred_element_type=F32
            )
            for t in range(4):
                value = res[0:channels, t * LANES : (t + 1) * LANES] + bias[arr, 0:channels]
                gating = res[channels:, t * LANES : (t + 1) * LANES] + bias[arr, channels:]
                pair_mask = mask * valid[row * ti + i0 + t].astype(F32)
                flip[pl.ds(4 * q + t, channels, stride=ci), :] = (
                    pair_mask * sigmoid(gating) * value
                )
            return 0

        lax.fori_loop(0, ci // 4, step, 0, unroll=True)

        def pack(p, _):
            for ch in range(nz):
                ab[arr, m, p, ch] = flip[
                    pl.ds(pl.multiple_of((p * nz + ch) * ci, ci), ci), :
                ].astype(BF16)
            return 0

        lax.fori_loop(0, nq, pack, 0, unroll=4)

    def gates(q, _):
        rows = nrm[pl.ds(4 * q, 4)].reshape(4 * LANES, cz)
        res = jnp.dot(rows, w_gate[...], preferred_element_type=F32) + b_gate[...]
        gate[pl.ds(4 * q, 4)] = sigmoid(res).reshape(4, LANES, cz)[:, 0:tj]
        return 0

    def wait_all(ref, sem):
        pltpu.make_async_copy(ref, ref, sem).wait()

    def send(src, dst, send_sem, recv_sem, device):
        pltpu.make_async_remote_copy(
            src_ref=src,
            dst_ref=dst,
            send_sem=send_sem,
            recv_sem=recv_sem,
            device_id=device,
            device_id_type=MESH,
        ).start()

    def send1(arr, m, src=None):
        src = ab.at[arr, m] if src is None else src

        def step(t, _):
            p = lax.rem(mine + t, nq)
            here = jnp.logical_and(p == mine, core == yl)

            @pl.when(here)
            def _():
                pltpu.make_async_copy(src.at[p], recv1.at[arr, m, col], r1.at[arr, m]).start()

            @pl.when(jnp.logical_not(here))
            def _():
                send(
                    src.at[p],
                    recv1.at[arr, m, col],
                    s1,
                    r1.at[arr, m],
                    (2 * z + p // nz, 2 * (p % nz) + yl),
                )

            return 0

        lax.fori_loop(0, nq, step, 0)

    far_first = sorted(range(nz), key=lambda place: -abs(shift[place]))

    def z_first():
        for place in far_first:
            src = ab.at[0, 0, :, lax.rem(z - place + ahead + nz, nz)]
            if shift[place]:
                send(src, zf.at[:, place], sz, rz, along(shift[place]))
            else:
                pltpu.make_async_copy(src, zf.at[:, place], rz).start()

    def then_plane():
        wait_all(zf, rz)
        send1(0, 0, zf)

    def enter(arr, m):
        wait_all(recv1.at[arr, m], r1.at[arr, m])

        at_site = (arr, m) == (0, 0)

        def step(place, _):
            block = place if at_site else lax.rem(z - place + ahead + nz, nz)
            for g in range(nq // 4):
                joined = join4([recv1[arr, m, 4 * g + n, block].astype(F32) for n in range(4)])
                for n in range(3):
                    lanes = slice((3 * g + n) * LANES, (3 * g + n + 1) * LANES)
                    if at_site:
                        za[place, core, 0:ci, lanes] = joined[n].astype(BF16)
                    else:
                        zs[arr, m, place, :, lanes] = joined[n].astype(BF16)
            return 0

        lax.fori_loop(0, nz, step, 0, unroll=2)
        if at_site:
            return
        for place in far_first:
            if arr == 0:
                dst = za.at[place, core, m * ci : (m + 1) * ci]
                sem = r2a.at[m]
            else:
                dst = zb.at[site_of[place], m, place]
                sem = r2b.at[m, site_of[place]]
            if shift[place]:
                send(zs.at[arr, m, place], dst, s2, sem, along(shift[place]))
            else:
                pltpu.make_async_copy(zs.at[arr, m, place], dst, sem).start()

    def held(site, m, e):
        return zb.at[site, m, group[e][0] : group[e][1]]

    passed = []

    def pass_on(m, s):
        for site in range(SITES):
            if s == 1:
                wait_all(held(site, m, site), r2b.at[m, site])
            for way, e, to in ((0, site - s + 1, site + 1), (1, site + s - 1, site - 1)):
                if 0 <= e < SITES and 0 <= to < SITES:
                    if s > 1:
                        wait_all(held(site, m, e), rf.at[m, s - 1, site, way])
                    send(
                        held(site, m, e),
                        held(to, m, e),
                        sf,
                        rf.at[m, s, to, way],
                        along(to - site),
                    )
                    passed.append((site, m, e))

    def swap(m):
        part = za.at[:, core, m * ci : (m + 1) * ci]
        return pltpu.make_async_remote_copy(
            src_ref=part,
            dst_ref=part,
            send_sem=so.at[m],
            recv_sem=ro.at[m],
            device_id=(row, 2 * w + 1 - core),
            device_id_type=MESH,
        )

    def product(m):
        for s in range(1, SITES):
            wait_all(held(SITES - 1, m, SITES - 1 - s), rf.at[m, s, SITES - 1, 0])
            wait_all(held(0, m, s), rf.at[m, s, 0, 1])
        for site in range(SITES):
            first, last = group[site]

            rows = (last - first) * 2 * ti
            res = lax.dot_general(
                za[first:last].reshape(rows, za.shape[-1]),
                zb[site, m].reshape(nz * ci, zb.shape[-1]),
                (((1,), (1,)), ((), ())),
                preferred_element_type=F32,
            )
            prods[m, first:last] = res.reshape(last - first, 2, ti, nz * ci).astype(BF16)
        if m < nch - 1:
            send_back(m)

    def send_back(m):
        for place in far_first:
            dst = back.at[m, lax.rem(z - site_of[place] + nz, nz)]
            if shift[place]:
                send(prods.at[m, place], dst, s3, r3.at[m], along(-shift[place]))
            else:
                pltpu.make_async_copy(prods.at[m, place], dst, r3.at[m]).start()

    def turn(m, load_block, store_block):
        def step(n, _):
            h, rows = n // 3, pl.ds(pl.multiple_of(n % 3 * 32, 32), 32)
            for i, block in enumerate(turn8([load_block(i, h, rows) for i in range(nz)])):
                store_block(i, h, rows, block.astype(BF16))
            return 0

        lax.fori_loop(0, 6, step, 0, unroll=2)

    def to_plane(m, dst, sem):
        def go(t, _):
            p = lax.rem(mine + 1 + t, nq)

            @pl.when(p == mine)
            def _():
                pltpu.make_async_copy(un.at[m, p], dst.at[mine], sem).start()

            @pl.when(p != mine)
            def _():
                device = (2 * z + p // nz, 2 * (p % nz) + core)
                send(un.at[m, p], dst.at[mine], s4, sem, device)

            return 0

        lax.fori_loop(0, nq, go, 0)

    def store_un(m):
        def store(i, h, rows, block):
            un[m, h * nz + i, rows] = block

        return store

    def turn_and_send(m):
        wait_all(back.at[m], r3.at[m])

        def load_block(ch, h, rows):
            block = back[m, ch, h, rows].astype(F32)
            return pltpu.roll(block, 16 * ((ch - ahead) % nz), 1) if ch != ahead else block

        turn(m, load_block, store_un(m))
        to_plane(m, land.at[m], r4.at[m])

    def turn_at_site(m):
        def load_block(place, h, rows):
            amount = 16 * lax.rem(z - site_of[place] - ahead + 2 * nz, nz)
            return pltpu.roll(prods[m, place, h, rows].astype(F32), amount, 1)

        turn(m, load_block, store_un(m))
        to_plane(m, mid, rm)

    def turn_and_return(m):
        wait_all(mid, rm)

        def load_block(n, half, rows):
            return mid[half * nz + n, rows].astype(F32)

        def store_block(place, half, rows, block):
            prods[m, place, half, rows] = block

        turn(m, load_block, store_block)
        send_back(m)

    def finish(m):
        late = m == nch - 1
        if late:
            wait_all(back.at[m], r3.at[m])
        else:
            wait_all(land.at[m], r4.at[m])
        gains, weights = (late_gain, w_late) if late else (out_gain, w_out)

        def block(p):
            return (back[m, p // 2, p % 2] if late else land[m, p]).astype(F32)

        total = jnp.zeros((ti, LANES), F32)
        for p in range(nq):
            total = total + block(p)
        mean = over_slots(total) * (1.0 / channels)
        total = jnp.zeros((ti, LANES), F32)
        for p in range(nq):
            centred = block(p) - mean
            total = total + centred * centred
        scale = lax.rsqrt(over_slots(total) * (1.0 / channels) + 1e-05)

        def scaled(p, _):
            y = (block(p) - mean) * scale * gains[pl.ds(p, 1), :]
            y = jnp.concatenate([y, jnp.zeros((LANES - ti, LANES), F32)], axis=0)
            flip[pl.ds(pl.multiple_of(p * LANES, LANES), LANES), :] = y.T
            return 0

        lax.fori_loop(0, nq, scaled, 0, unroll=True)

        def mix(j, _):
            normal = flip[pl.ds(j, channels, stride=ci), :].astype(BF16)
            linear = lax.dot_general(
                normal, weights[...], (((0,), (0,)), ((), ())), preferred_element_type=F32
            )
            flop[pl.ds(j, ti, stride=ci), :] = linear[0:ti]
            return 0

        lax.fori_loop(0, ci, mix, 0, unroll=True)

        def emit(n, _):
            rows, columns = pl.ds(8 * n, 8), slice(m * ci, (m + 1) * ci)
            linear = flop[pl.ds(pl.multiple_of(8 * n * ci, 8 * ci), 8 * ci), :] + b_out[...]
            update[rows, columns, :] = (
                linear.reshape(8, ci, cz) * gate[rows, columns, :]
            ).astype(BF16)
            return 0

        lax.fori_loop(0, ti // 8, emit, 0, unroll=2)

    def join_swap(m):
        if m:
            wait_all(za.at[:, core, m * ci : (m + 1) * ci], r2a.at[m])
        swap(m).start()

    def all_gates():
        lax.fori_loop(0, ti // 4, gates, 0, unroll=2)

    def all_of_a():
        for m in range(nch):
            swap(m).wait_recv()

    first = [(0, 0), (1, 0)]
    load.wait()
    for chunk in first:
        front(*chunk)
    pl.semaphore_wait(barrier, 2 * nq - 1 + 2 * ahead)
    plan = [
        (z_first,),
        (send1, 1, 0),
        (front, 0, 1),
        (send1, 0, 1),
        (front, 1, 1),
        (send1, 1, 1),
        (front, 0, 2),
        (enter, 1, 0),
        (send1, 0, 2),
        (front, 0, 3),
        (then_plane,),
        (front, 1, 2),
        (enter, 0, 1),
        (send1, 0, 3),
        (front, 0, 4),
        (pass_on, 0, 1),
        (enter, 1, 1),
        (send1, 1, 2),
        (front, 0, 5),
        (enter, 0, 2),
        (send1, 0, 4),
        (enter, 0, 0),
        (join_swap, 0),
        (join_swap, 1),
        (front, 1, 3),
        (pass_on, 1, 1),
        (enter, 0, 3),
        (send1, 0, 5),
        (front, 1, 4),
        (join_swap, 2),
        (all_gates,),
        (enter, 1, 2),
        (send1, 1, 3),
        (front, 1, 5),
        (enter, 0, 4),
        (send1, 1, 4),
        (join_swap, 3),
        (enter, 0, 5),
        (send1, 1, 5),
        (pass_on, 2, 1),
        (enter, 1, 3),
        (join_swap, 4),
        (enter, 1, 4),
        (join_swap, 5),
        (enter, 1, 5),
        (all_of_a,),
        (product, 0),
        (product, 1),
        (pass_on, 3, 1),
        (product, 2),
        (pass_on, 4, 1),
        (pass_on, 5, 1),
        (turn_and_send, 0),
        (turn_and_send, 1),
        (finish, 0),
        (turn_and_send, 2),
        (product, 3),
        (product, 4),
        (finish, 1),
        (product, 5),
        (turn_at_site, 5),
        (finish, 2),
        (turn_and_send, 3),
        (turn_and_return, 5),
        (turn_and_send, 4),
        (finish, 3),
        (finish, 4),
        (finish, 5),
    ]
    for act, *which in plan:
        act(*which)

    for arr in range(2):
        for m in range(nch):

            @pl.when(core == yl)
            def _():
                wait_all(ab.at[arr, m, 0 : nq - 1], s1)

            @pl.when(core != yl)
            def _():
                wait_all(ab.at[arr, m], s1)

            if (arr, m) != (0, 0):
                wait_all(zs.at[arr, m, 0:n_remote], s2)
    wait_all(zf.at[:, 0:n_remote], sz)
    for site, m, e in passed:
        wait_all(held(site, m, e), sf)
    for m in range(nch):
        swap(m).wait_send()
        wait_all(prods.at[m, 0:n_remote], s3)
        wait_all(un.at[m, 0 : nq - 1], s4)


def local(pair, residue_mask, norm_gain, w_in, b_in, w_gate, b_gate, out_gain, w_out, b_out):
    ti, tj, cz = pair.shape
    channels = w_in.shape[1] // 4
    nz = lax.axis_size("row") // 2
    nq = 2 * nz
    ci = CHUNK
    nch = ti // ci
    depth = nq * ti
    sem = pltpu.SemaphoreType.DMA
    vmem = pl.BlockSpec(memory_space=pltpu.VMEM)
    smem = pl.BlockSpec(memory_space=pltpu.SMEM)
    return pl.pallas_call(
        functools.partial(triangle_kernel, nz),
        out_shape=jax.ShapeDtypeStruct((ti, tj, cz), BF16),
        in_specs=[pl.BlockSpec(memory_space=pl.ANY), smem] + [vmem] * 5 + [smem] + [vmem] * 2,
        out_specs=vmem,
        scratch_shapes=[
            pltpu.VMEM((ti, tj, cz), BF16),
            sem,
            pltpu.VMEM((ti, LANES, cz), BF16),
            pltpu.VMEM((2, 2 * channels, cz), BF16),
            pltpu.VMEM((2, 2 * channels, LANES), F32),
            pltpu.VMEM((ti, tj, cz), F32),
            pltpu.VMEM((channels * ci, LANES), F32),
            pltpu.VMEM((ti * ci, cz), F32),
            pltpu.VMEM((nq, LANES), F32),
            pltpu.VMEM((nq, LANES), F32),
            pltpu.VMEM((channels, cz), BF16),
            pltpu.VMEM((2, nch, nq, nz, ci, LANES), BF16),
            pltpu.VMEM((nq, nz, ci, LANES), BF16),
            pltpu.VMEM((2, nch, nq, nz, ci, LANES), BF16),
            pltpu.VMEM((2, nch, nz, ci, depth), BF16),
            pltpu.VMEM((nz, 2, ti, depth), BF16),
            pltpu.VMEM((SITES, nch, nz, ci, depth), BF16),
            pltpu.VMEM((nch, nz, 2, ti, nz * ci), BF16),
            pltpu.VMEM((nch, nz, 2, ti, nz * ci), BF16),
            pltpu.VMEM((nch, nq, ti, LANES), BF16),
            pltpu.VMEM((nch, nq, ti, LANES), BF16),
            pltpu.VMEM((nq, ti, LANES), BF16),
            sem,
            sem,
            sem((2, nch)),
            sem,
            sem,
            sem,
            sem((nch,)),
            sem((nch, SITES)),
            sem,
            sem((nch, SITES, SITES, 2)),
            sem((nch,)),
            sem((nch,)),
            sem,
            sem((nch,)),
            sem,
            sem((nch,)),
        ],
        compiler_params=pltpu.CompilerParams(
            collective_id=0, has_side_effects=True, vmem_limit_bytes=60 * 2**20
        ),
    )(
        pair,
        residue_mask,
        norm_gain.reshape(1, cz),
        w_in,
        b_in.reshape(1, 4 * channels),
        w_gate,
        b_gate.reshape(1, cz),
        out_gain,
        w_out,
        b_out.reshape(1, cz),
    )


def solution(mesh):
    in_specs = (P("row", "col", None), P(), P(), P(), P(), P(), P(), P(), P(), P())
    out_specs = P("row", "col", None)
    return jax.shard_map(local, mesh=mesh, in_specs=in_specs, out_specs=out_specs, check_vma=False)
```

```python
import functools

import jax
import jax.numpy as jnp
from jax import lax
from jax.experimental import pallas as pl
from jax.experimental.pallas import tpu as pltpu
from jax.sharding import PartitionSpec as P

MESH = pl.DeviceIdType.MESH
BF16 = jnp.bfloat16
F32 = jnp.float32
LANES = 128
CHUNK = 16
SITES = 2


def sigmoid(x):
    return 0.5 * jnp.tanh(0.5 * x) + 0.5


def join4(parts):
    lane = lax.broadcasted_iota(jnp.int32, parts[0].shape, 1)
    one, two, three = (pltpu.roll(parts[n], 128 - 32 * n, 1) for n in (1, 2, 3))
    return (
        jnp.where(lane < 96, parts[0], one),
        jnp.where(lane < 64, one, two),
        jnp.where(lane < 32, two, three),
    )


def turn8(parts):
    slot = lax.broadcasted_iota(jnp.int32, parts[0].shape, 1) // 16
    for step in (1, 2, 4):
        low = (slot // step) % 2 == 0
        turned = list(parts)
        for i in range(8):
            if not i & step:
                first, second = parts[i], parts[i | step]
                turned[i] = jnp.where(low, first, pltpu.roll(second, 16 * step, 1))
                turned[i | step] = jnp.where(low, pltpu.roll(first, 128 - 16 * step, 1), second)
        parts = turned
    return parts


def over_slots(x):
    for step in (16, 32, 64):
        x = x + pltpu.roll(x, step, 1)
    return x


def triangle_kernel(
    nz,
    pair_in,
    valid,
    norm_gain,
    w_in,
    b_in,
    w_gate,
    b_gate,
    gain,
    w_out,
    b_out,
    update,
    pair,
    sp,
    nrm,
    wt,
    bias,
    gate,
    flip,
    flop,
    out_gain,
    late_gain,
    w_late,
    ab,
    zf,
    recv1,
    zs,
    za,
    zb,
    prods,
    back,
    un,
    land,
    mid,
    rm,
    s1,
    r1,
    sz,
    rz,
    s2,
    r2a,
    r2b,
    sf,
    rf,
    so,
    ro,
    s3,
    r3,
    s4,
    r4,
):
    nq = 2 * nz
    ci = CHUNK
    channels = nq * nz
    ti, tj, cz = pair.shape
    nch = ti // ci
    row, col = lax.axis_index("row"), lax.axis_index("col")
    z, yl = row // 2, row % 2
    w, core = col // 2, col % 2
    mine = yl * nz + w

    ahead = (nz - SITES) // 2
    site_of = [min(max(place - ahead, 0), SITES - 1) for place in range(nz)]
    group = [(site_of.index(e), site_of.index(e) + site_of.count(e)) for e in range(SITES)]
    shift = [site_of[place] - place + ahead for place in range(nz)]
    n_remote = sum(1 for d in shift if d)

    def along(d):
        return (2 * lax.rem(z + (d + nz) % nz, nz) + yl, col)

    barrier = pltpu.get_barrier_semaphore()

    def greet_plane(t, _):
        dev = lax.rem(yl * nq + col + t, 2 * nq)
        pl.semaphore_signal(
            barrier, inc=1, device_id=(2 * z + dev // nq, dev % nq), device_id_type=MESH
        )
        return 0

    lax.fori_loop(1, 2 * nq, greet_plane, 0)
    for d in range(1, ahead + 1):
        for sign in (1, -1):
            pl.semaphore_signal(barrier, inc=1, device_id=along(sign * d), device_id_type=MESH)

    load = pltpu.make_async_copy(pair_in, pair, sp)
    load.start()

    turned = w_in[...].astype(F32).T.astype(BF16)
    column = jnp.broadcast_to(b_in[...], (LANES, 4 * channels)).T
    for arr in range(2):
        wt[arr] = turned[2 * arr * channels : 2 * (arr + 1) * channels]
        bias[arr] = column[2 * arr * channels : 2 * (arr + 1) * channels]
    nrm[:, tj:, :] = jnp.zeros((ti, LANES - tj, cz), BF16)
    lane = lax.broadcasted_iota(jnp.int32, (1, LANES), 1)

    def col_valid(j, mask):
        return jnp.where(lane == j, valid[col * tj + j].astype(F32), mask)

    mask = lax.fori_loop(0, tj, col_valid, jnp.zeros((1, LANES), F32), unroll=8)

    def spread(p, _):
        line = jnp.zeros((1, LANES), F32)
        for ch in range(nz):
            line = jnp.where(lane // ci == ch, gain[p * nz + ch], line)
        out_gain[pl.ds(p, 1), :] = line
        line = jnp.zeros((1, LANES), F32)
        for n in range(nz):
            line = jnp.where(lane // ci == n, gain[(p % 2 * nz + n) * nz + p // 2], line)
        late_gain[pl.ds(p, 1), :] = line
        return 0

    lax.fori_loop(0, nq, spread, 0)
    flop[0:channels, :] = w_out[...].astype(F32)
    for ch in range(nz):
        w_late[ch * nq : (ch + 1) * nq] = flop[pl.ds(ch, nq, stride=nz), :].astype(BF16)
    normed = set()

    def front(arr, m):
        fresh = m not in normed
        normed.add(m)

        def step(q, _):
            i0 = m * ci + 4 * q
            if fresh:
                x = pair[pl.ds(i0, 4)].astype(F32)
                centred = x - jnp.mean(x, axis=-1, keepdims=True)
                var = jnp.mean(centred * centred, axis=-1, keepdims=True)
                y = centred * lax.rsqrt(var + 1e-05) * norm_gain[...].reshape(1, 1, cz)
                nrm[pl.ds(i0, 4), 0:tj, :] = y.astype(BF16)
            rhs = nrm[pl.ds(i0, 4)].reshape(4 * LANES, cz)
            res = lax.dot_general(
                wt[arr], rhs, (((1,), (1,)), ((), ())), preferred_element_type=F32
            )
            for t in range(4):
                value = res[0:channels, t * LANES : (t + 1) * LANES] + bias[arr, 0:channels]
                gating = res[channels:, t * LANES : (t + 1) * LANES] + bias[arr, channels:]
                pair_mask = mask * valid[row * ti + i0 + t].astype(F32)
                flip[pl.ds(4 * q + t, channels, stride=ci), :] = (
                    pair_mask * sigmoid(gating) * value
                )
            return 0

        lax.fori_loop(0, ci // 4, step, 0, unroll=True)

        def pack(p, _):
            for ch in range(nz):
                ab[arr, m, p, ch] = flip[
                    pl.ds(pl.multiple_of((p * nz + ch) * ci, ci), ci), :
                ].astype(BF16)
            return 0

        lax.fori_loop(0, nq, pack, 0, unroll=4)

    def gates(q, _):
        rows = nrm[pl.ds(4 * q, 4)].reshape(4 * LANES, cz)
        res = jnp.dot(rows, w_gate[...], preferred_element_type=F32) + b_gate[...]
        gate[pl.ds(4 * q, 4)] = sigmoid(res).reshape(4, LANES, cz)[:, 0:tj]
        return 0

    def wait_all(ref, sem):
        pltpu.make_async_copy(ref, ref, sem).wait()

    def send(src, dst, send_sem, recv_sem, device):
        pltpu.make_async_remote_copy(
            src_ref=src,
            dst_ref=dst,
            send_sem=send_sem,
            recv_sem=recv_sem,
            device_id=device,
            device_id_type=MESH,
        ).start()

    def send1(arr, m, src=None):
        src = ab.at[arr, m] if src is None else src

        def step(t, _):
            p = lax.rem(mine + t, nq)
            here = jnp.logical_and(p == mine, core == yl)

            @pl.when(here)
            def _():
                pltpu.make_async_copy(src.at[p], recv1.at[arr, m, col], r1.at[arr, m]).start()

            @pl.when(jnp.logical_not(here))
            def _():
                send(
                    src.at[p],
                    recv1.at[arr, m, col],
                    s1,
                    r1.at[arr, m],
                    (2 * z + p // nz, 2 * (p % nz) + yl),
                )

            return 0

        lax.fori_loop(0, nq, step, 0)

    far_first = sorted(range(nz), key=lambda place: -abs(shift[place]))

    def z_first():
        for place in far_first:
            src = ab.at[0, 0, :, lax.rem(z - place + ahead + nz, nz)]
            if shift[place]:
                send(src, zf.at[:, place], sz, rz, along(shift[place]))
            else:
                pltpu.make_async_copy(src, zf.at[:, place], rz).start()

    def then_plane():
        wait_all(zf, rz)
        send1(0, 0, zf)

    def enter(arr, m):
        wait_all(recv1.at[arr, m], r1.at[arr, m])

        at_site = (arr, m) == (0, 0)

        def step(place, _):
            block = place if at_site else lax.rem(z - place + ahead + nz, nz)
            for g in range(nq // 4):
                joined = join4([recv1[arr, m, 4 * g + n, block].astype(F32) for n in range(4)])
                for n in range(3):
                    lanes = slice((3 * g + n) * LANES, (3 * g + n + 1) * LANES)
                    if at_site:
                        za[place, core, 0:ci, lanes] = joined[n].astype(BF16)
                    else:
                        zs[arr, m, place, :, lanes] = joined[n].astype(BF16)
            return 0

        lax.fori_loop(0, nz, step, 0, unroll=2)
        if at_site:
            return
        for place in far_first:
            if arr == 0:
                dst = za.at[place, core, m * ci : (m + 1) * ci]
                sem = r2a.at[m]
            else:
                dst = zb.at[site_of[place], m, place]
                sem = r2b.at[m, site_of[place]]
            if shift[place]:
                send(zs.at[arr, m, place], dst, s2, sem, along(shift[place]))
            else:
                pltpu.make_async_copy(zs.at[arr, m, place], dst, sem).start()

    def held(site, m, e):
        return zb.at[site, m, group[e][0] : group[e][1]]

    passed = []

    def pass_on(m, s):
        for site in range(SITES):
            if s == 1:
                wait_all(held(site, m, site), r2b.at[m, site])
            for way, e, to in ((0, site - s + 1, site + 1), (1, site + s - 1, site - 1)):
                if 0 <= e < SITES and 0 <= to < SITES:
                    if s > 1:
                        wait_all(held(site, m, e), rf.at[m, s - 1, site, way])
                    send(
                        held(site, m, e),
                        held(to, m, e),
                        sf,
                        rf.at[m, s, to, way],
                        along(to - site),
                    )
                    passed.append((site, m, e))

    def swap(m):
        part = za.at[:, core, m * ci : (m + 1) * ci]
        return pltpu.make_async_remote_copy(
            src_ref=part,
            dst_ref=part,
            send_sem=so.at[m],
            recv_sem=ro.at[m],
            device_id=(row, 2 * w + 1 - core),
            device_id_type=MESH,
        )

    def product(m):
        for s in range(1, SITES):
            wait_all(held(SITES - 1, m, SITES - 1 - s), rf.at[m, s, SITES - 1, 0])
            wait_all(held(0, m, s), rf.at[m, s, 0, 1])
        for site in range(SITES):
            first, last = group[site]

            rows = (last - first) * 2 * ti
            res = lax.dot_general(
                za[first:last].reshape(rows, za.shape[-1]),
                zb[site, m].reshape(nz * ci, zb.shape[-1]),
                (((1,), (1,)), ((), ())),
                preferred_element_type=F32,
            )
            prods[m, first:last] = res.reshape(last - first, 2, ti, nz * ci).astype(BF16)
        if m < nch - 1:
            send_back(m)

    def send_back(m):
        for place in far_first:
            dst = back.at[m, lax.rem(z - site_of[place] + nz, nz)]
            if shift[place]:
                send(prods.at[m, place], dst, s3, r3.at[m], along(-shift[place]))
            else:
                pltpu.make_async_copy(prods.at[m, place], dst, r3.at[m]).start()

    def turn(m, load_block, store_block):
        def step(n, _):
            h, rows = n // 3, pl.ds(pl.multiple_of(n % 3 * 32, 32), 32)
            for i, block in enumerate(turn8([load_block(i, h, rows) for i in range(nz)])):
                store_block(i, h, rows, block.astype(BF16))
            return 0

        lax.fori_loop(0, 6, step, 0, unroll=2)

    def to_plane(m, dst, sem):
        def go(t, _):
            p = lax.rem(mine + 1 + t, nq)

            @pl.when(p == mine)
            def _():
                pltpu.make_async_copy(un.at[m, p], dst.at[mine], sem).start()

            @pl.when(p != mine)
            def _():
                device = (2 * z + p // nz, 2 * (p % nz) + core)
                send(un.at[m, p], dst.at[mine], s4, sem, device)

            return 0

        lax.fori_loop(0, nq, go, 0)

    def store_un(m):
        def store(i, h, rows, block):
            un[m, h * nz + i, rows] = block

        return store

    def turn_and_send(m):
        wait_all(back.at[m], r3.at[m])

        def load_block(ch, h, rows):
            block = back[m, ch, h, rows].astype(F32)
            return pltpu.roll(block, 16 * ((ch - ahead) % nz), 1) if ch != ahead else block

        turn(m, load_block, store_un(m))
        to_plane(m, land.at[m], r4.at[m])

    def turn_at_site(m):
        def load_block(place, h, rows):
            amount = 16 * lax.rem(z - site_of[place] - ahead + 2 * nz, nz)
            return pltpu.roll(prods[m, place, h, rows].astype(F32), amount, 1)

        turn(m, load_block, store_un(m))
        to_plane(m, mid, rm)

    def turn_and_return(m):
        wait_all(mid, rm)

        def load_block(n, half, rows):
            return mid[half * nz + n, rows].astype(F32)

        def store_block(place, half, rows, block):
            prods[m, place, half, rows] = block

        turn(m, load_block, store_block)
        send_back(m)

    def finish(m):
        late = m == nch - 1
        if late:
            wait_all(back.at[m], r3.at[m])
        else:
            wait_all(land.at[m], r4.at[m])
        gains, weights = (late_gain, w_late) if late else (out_gain, w_out)

        def block(p):
            return (back[m, p // 2, p % 2] if late else land[m, p]).astype(F32)

        total = jnp.zeros((ti, LANES), F32)
        for p in range(nq):
            total = total + block(p)
        mean = over_slots(total) * (1.0 / channels)
        total = jnp.zeros((ti, LANES), F32)
        for p in range(nq):
            centred = block(p) - mean
            total = total + centred * centred
        scale = lax.rsqrt(over_slots(total) * (1.0 / channels) + 1e-05)

        def scaled(p, _):
            y = (block(p) - mean) * scale * gains[pl.ds(p, 1), :]
            y = jnp.concatenate([y, jnp.zeros((LANES - ti, LANES), F32)], axis=0)
            flip[pl.ds(pl.multiple_of(p * LANES, LANES), LANES), :] = y.T
            return 0

        lax.fori_loop(0, nq, scaled, 0, unroll=True)

        def mix(j, _):
            normal = flip[pl.ds(j, channels, stride=ci), :].astype(BF16)
            linear = lax.dot_general(
                normal, weights[...], (((0,), (0,)), ((), ())), preferred_element_type=F32
            )
            flop[pl.ds(j, ti, stride=ci), :] = linear[0:ti]
            return 0

        lax.fori_loop(0, ci, mix, 0, unroll=True)

        def emit(n, _):
            rows, columns = pl.ds(8 * n, 8), slice(m * ci, (m + 1) * ci)
            linear = flop[pl.ds(pl.multiple_of(8 * n * ci, 8 * ci), 8 * ci), :] + b_out[...]
            update[rows, columns, :] = (
                linear.reshape(8, ci, cz) * gate[rows, columns, :]
            ).astype(BF16)
            return 0

        lax.fori_loop(0, ti // 8, emit, 0, unroll=2)

    def join_swap(m):
        if m:
            wait_all(za.at[:, core, m * ci : (m + 1) * ci], r2a.at[m])
        swap(m).start()

    def all_gates():
        lax.fori_loop(0, ti // 4, gates, 0, unroll=2)

    def all_of_a():
        for m in range(nch):
            swap(m).wait_recv()

    first = [(0, 0), (1, 0)]
    load.wait()
    for chunk in first:
        front(*chunk)
    pl.semaphore_wait(barrier, 2 * nq - 1 + 2 * ahead)
    plan = [
        (z_first,),
        (send1, 1, 0),
        (front, 0, 1),
        (send1, 0, 1),
        (front, 1, 1),
        (send1, 1, 1),
        (front, 0, 2),
        (enter, 1, 0),
        (send1, 0, 2),
        (front, 0, 3),
        (then_plane,),
        (front, 1, 2),
        (enter, 0, 1),
        (send1, 0, 3),
        (front, 0, 4),
        (pass_on, 0, 1),
        (enter, 1, 1),
        (send1, 1, 2),
        (front, 0, 5),
        (enter, 0, 2),
        (send1, 0, 4),
        (enter, 0, 0),
        (join_swap, 0),
        (join_swap, 1),
        (front, 1, 3),
        (pass_on, 1, 1),
        (enter, 0, 3),
        (send1, 0, 5),
        (front, 1, 4),
        (join_swap, 2),
        (all_gates,),
        (enter, 1, 2),
        (send1, 1, 3),
        (front, 1, 5),
        (enter, 0, 4),
        (send1, 1, 4),
        (join_swap, 3),
        (enter, 0, 5),
        (send1, 1, 5),
        (pass_on, 2, 1),
        (enter, 1, 3),
        (join_swap, 4),
        (enter, 1, 4),
        (join_swap, 5),
        (enter, 1, 5),
        (all_of_a,),
        (product, 0),
        (product, 1),
        (pass_on, 3, 1),
        (product, 2),
        (pass_on, 4, 1),
        (pass_on, 5, 1),
        (turn_and_send, 0),
        (turn_and_send, 1),
        (finish, 0),
        (turn_and_send, 2),
        (product, 3),
        (product, 4),
        (finish, 1),
        (product, 5),
        (turn_at_site, 5),
        (finish, 2),
        (turn_and_send, 3),
        (turn_and_return, 5),
        (turn_and_send, 4),
        (finish, 3),
        (finish, 4),
        (finish, 5),
    ]
    for act, *which in plan:
        act(*which)

    for arr in range(2):
        for m in range(nch):

            @pl.when(core == yl)
            def _():
                wait_all(ab.at[arr, m, 0 : nq - 1], s1)

            @pl.when(core != yl)
            def _():
                wait_all(ab.at[arr, m], s1)

            if (arr, m) != (0, 0):
                wait_all(zs.at[arr, m, 0:n_remote], s2)
    wait_all(zf.at[:, 0:n_remote], sz)
    for site, m, e in passed:
        wait_all(held(site, m, e), sf)
    for m in range(nch):
        swap(m).wait_send()
        wait_all(prods.at[m, 0:n_remote], s3)
        wait_all(un.at[m, 0 : nq - 1], s4)


def local(pair, residue_mask, norm_gain, w_in, b_in, w_gate, b_gate, out_gain, w_out, b_out):
    ti, tj, cz = pair.shape
    channels = w_in.shape[1] // 4
    nz = lax.axis_size("row") // 2
    nq = 2 * nz
    ci = CHUNK
    nch = ti // ci
    depth = nq * ti
    sem = pltpu.SemaphoreType.DMA
    vmem = pl.BlockSpec(memory_space=pltpu.VMEM)
    smem = pl.BlockSpec(memory_space=pltpu.SMEM)
    return pl.pallas_call(
        functools.partial(triangle_kernel, nz),
        out_shape=jax.ShapeDtypeStruct((ti, tj, cz), BF16),
        in_specs=[pl.BlockSpec(memory_space=pl.ANY), smem] + [vmem] * 5 + [smem] + [vmem] * 2,
        out_specs=vmem,
        scratch_shapes=[
            pltpu.VMEM((ti, tj, cz), BF16),
            sem,
            pltpu.VMEM((ti, LANES, cz), BF16),
            pltpu.VMEM((2, 2 * channels, cz), BF16),
            pltpu.VMEM((2, 2 * channels, LANES), F32),
            pltpu.VMEM((ti, tj, cz), F32),
            pltpu.VMEM(((channels + 1) * ci, LANES), F32),
            pltpu.VMEM(((ti + 1) * ci, cz), F32),
            pltpu.VMEM((nq, LANES), F32),
            pltpu.VMEM((nq, LANES), F32),
            pltpu.VMEM((channels, cz), BF16),
            pltpu.VMEM((2, nch, nq, nz, ci, LANES), BF16),
            pltpu.VMEM((nq, nz, ci, LANES), BF16),
            pltpu.VMEM((2, nch, nq, nz, ci, LANES), BF16),
            pltpu.VMEM((2, nch, nz, ci, depth), BF16),
            pltpu.VMEM((nz, 2, ti, depth), BF16),
            pltpu.VMEM((SITES, nch, nz, ci, depth), BF16),
            pltpu.VMEM((nch, nz, 2, ti, nz * ci), BF16),
            pltpu.VMEM((nch, nz, 2, ti, nz * ci), BF16),
            pltpu.VMEM((nch, nq, ti, LANES), BF16),
            pltpu.VMEM((nch, nq, ti, LANES), BF16),
            pltpu.VMEM((nq, ti, LANES), BF16),
            sem,
            sem,
            sem((2, nch)),
            sem,
            sem,
            sem,
            sem((nch,)),
            sem((nch, SITES)),
            sem,
            sem((nch, SITES, SITES, 2)),
            sem((nch,)),
            sem((nch,)),
            sem,
            sem((nch,)),
            sem,
            sem((nch,)),
        ],
        compiler_params=pltpu.CompilerParams(
            collective_id=0, has_side_effects=True, vmem_limit_bytes=60 * 2**20
        ),
    )(
        pair,
        residue_mask,
        norm_gain.reshape(1, cz),
        w_in,
        b_in.reshape(1, 4 * channels),
        w_gate,
        b_gate.reshape(1, cz),
        out_gain,
        w_out,
        b_out.reshape(1, cz),
    )


def solution(mesh):
    in_specs = (P("row", "col", None), P(), P(), P(), P(), P(), P(), P(), P(), P())
    out_specs = P("row", "col", None)
    return jax.shard_map(local, mesh=mesh, in_specs=in_specs, out_specs=out_specs, check_vma=False)
```
